512 devices in a mesh: tok: 32 (over x_lo, z), feat: 16 (over y, x_hi, core).
Axes of the slice: x: 4 (x_hi: 2, x_lo: 2; x = x_hi * 2 + x_lo), y: 4, z: 16, core: 2. Of those that a mesh axis runs over, the one named last changes fastest.
Arguments:
- activations: float32 [65536, 8192], P('tok', 'feat'), may hold values from -200 to 200, as said below
- sketch: float32 [8192, 128], P('feat'), may hold values from -0.0625 to 0.0625
Outputs:
- first_basis: float32 [65536, 128], P(('tok', 'feat'))
- range_basis: float32 [65536, 128], P(('tok', 'feat'))
- triangle: float32 [128, 128], replicated
The draws below stay inside these ranges and needn't reach their ends.
Inputs may be any that keep to these rules, and one draw needn't show every extreme that they name: activations of one layer, real valued.
All inputs are finite; a program needn't handle non-finite values.
Results may differ from the reference program's by a relative error of at most 0.000078.
Values sent between devices are 32-bit elements; how exact they have to be, the bound alone decides.
No kernel may reach another device: no remote copies, remote signals or barrier semaphores. Data moves between devices by JAX's collectives and lax.ppermute only.
A program may use at most 64 MiB of HBM per device.

```python
import math
import jax
import jax.numpy as jnp
from jax import lax

D = 8192
K = 128
TOKENS = 65536


def draw_activations(key, part):
    key = jax.random.fold_in(key, 11)
    key_base, key_rows, key_cols = jax.random.split(key, 3)
    base = jnp.clip(jax.random.normal(key_base, (TOKENS, D), jnp.float32), -6.0, 6.0)
    row_scale = jnp.exp(jax.random.uniform(key_rows, (TOKENS, 1), jnp.float32) * math.log(10.0))
    col_scale = jnp.exp(jax.random.uniform(key_cols, (1, D), jnp.float32) * math.log(10.0))
    return base * row_scale * col_scale / 3.0


def block_scale(key, extent, cuts, least, largest):
    loudness, own = 1.0, jax.random.fold_in(key, 6)
    for position, blocks in cuts:
        steps = jnp.exp(jax.random.uniform(jax.random.fold_in(own, position), (blocks,), jnp.float32, least / len(cuts), largest / len(cuts)))
        loudness = loudness * jnp.repeat(steps, extent[position] // blocks).reshape([-1 if axis == position else 1 for axis in range(len(extent))])
    return loudness


def centred(rng, shape, width, reach, pieces=(), kind=jnp.bfloat16):
    values = jax.random.normal(rng, shape, jnp.float32) * width
    if len(pieces) > 0:
        values = block_scale(rng, shape, pieces, -0.22, 0.18) * values
    return jnp.clip(values, min=-reach, max=reach).astype(kind)


def setup_inputs(seed: int = 0) -> dict:
    keys = jax.random.split(jax.random.key(seed), 3)
    activations = draw_activations(jax.random.fold_in(keys[2], 71), 0)
    sketch = centred(keys[1], (D, K), D ** -0.5, 0.0625, ((0, 16),), jnp.float32)
    return {"activations": activations, "sketch": sketch}


TOP = lax.Precision.HIGHEST

def product(left_side, right_side):
    return jnp.dot(left_side.astype(jnp.float32), right_side.astype(jnp.float32), precision=TOP, preferred_element_type=jnp.float32)

def inner_product(left_side, right_side):
    return lax.dot_general(left_side.astype(jnp.float32), right_side.astype(jnp.float32), (((0,), (0,)), ((), ())), precision=TOP, preferred_element_type=jnp.float32)

def orthonormal(matrix):
    gram_matrix = inner_product(matrix, matrix)
    lower_factor = jnp.linalg.cholesky(gram_matrix)
    identity = jnp.eye(gram_matrix.shape[0], dtype=jnp.float32)
    inverse = jax.scipy.linalg.solve_triangular(lower_factor, identity, lower=True)
    return (product(matrix, inverse.T), lower_factor)

def reference(activations, sketch):
    image = product(activations, sketch)
    first_basis, unused_first = orthonormal(image)
    back_image = inner_product(activations, first_basis)
    weights, unused_back = orthonormal(back_image)
    range_image = product(activations, weights)
    range_basis, lower_factor = orthonormal(range_image)
    triangle = lower_factor / jnp.sqrt(jnp.float32(TOKENS))
    return (first_basis, range_basis, triangle)
```

```python
import jax
import jax.numpy as jnp
from jax import lax
from jax.sharding import PartitionSpec as P

TOP = lax.Precision.HIGHEST


def product(left_side, right_side):
    return jnp.dot(left_side, right_side, precision=TOP, preferred_element_type=jnp.float32)


def inner_product(left_side, right_side):
    return lax.dot_general(
        left_side,
        right_side,
        (((0,), (0,)), ((), ())),
        precision=TOP,
        preferred_element_type=jnp.float32,
    )


def factor(gram_matrix):
    lower_factor = jnp.linalg.cholesky(gram_matrix)
    identity = jnp.eye(gram_matrix.shape[0], dtype=jnp.float32)
    inverse = jax.scipy.linalg.solve_triangular(lower_factor, identity, lower=True)
    return (lower_factor, inverse)


def scatter_sum(parts, axis):
    return jnp.sum(lax.all_to_all(parts, axis, 0, 0), axis=0)


def gather(block, axis):
    count = lax.axis_size(axis)
    return lax.all_to_all(jnp.broadcast_to(block[None], (count,) + block.shape), axis, 0, 0)


def per_device(activations, sketch):
    row_count, column_count = activations.shape
    width = sketch.shape[1]
    tok_count = lax.axis_size("tok")
    feat_count = lax.axis_size("feat")
    row_block = row_count // feat_count
    image_part = product(activations, sketch)
    image_block = scatter_sum(image_part.reshape(feat_count, row_block, width), "feat")
    image = gather(image_block, "feat").reshape(row_count, width)
    back_part = inner_product(activations, image).reshape(tok_count, -1, width)
    gram_part = inner_product(image, image).reshape(tok_count, -1, width)
    back_rows = back_part.shape[1]
    gram_rows = gram_part.shape[1]
    sums = scatter_sum(jnp.concatenate([back_part, gram_part], axis=1), "tok")
    both = gather(sums, "tok")
    back_raw = both[:, :back_rows].reshape(column_count, width)
    gram_first = both[:, back_rows:].reshape(width, width)
    unused_first, inverse_first = factor(gram_first)
    first_block = product(image_block, inverse_first.T)
    back_image = product(back_raw, inverse_first.T)
    range_part = product(activations, back_image).reshape(feat_count, row_block, width)
    gram_part = inner_product(back_image, back_image).reshape(feat_count, -1, width)
    gram_rows = gram_part.shape[1]
    sums = scatter_sum(jnp.concatenate([range_part, gram_part], axis=1), "feat")
    gram_back = gather(sums[row_block:], "feat").reshape(width, width)
    unused_back, inverse_back = factor(gram_back)
    range_block = product(sums[:row_block], inverse_back.T)
    gram_part = inner_product(range_block, range_block).reshape(feat_count, -1, width)
    gram_slice = scatter_sum(gram_part, "feat")
    gram_slice = jnp.sum(gather(gram_slice, "tok"), axis=0)
    gram_last = gather(gram_slice, "feat").reshape(width, width)
    lower_factor, inverse_last = factor(gram_last)
    range_basis = product(range_block, inverse_last.T)
    triangle = lower_factor / jnp.sqrt(jnp.float32(row_count * tok_count))
    return (first_block, range_basis, triangle)


def solution(mesh):
    return jax.shard_map(
        per_device,
        mesh=mesh,
        in_specs=(P("tok", "feat"), P("feat", None)),
        out_specs=(P(("tok", "feat"), None), P(("tok", "feat"), None), P()),
        check_vma=False,
    )
```

```python
import jax
import jax.numpy as jnp
from jax import lax
from jax.experimental import pallas as pl
from jax.sharding import Mesh, PartitionSpec as P

TOP = lax.Precision.HIGHEST
PANEL = 8
SWAP = [(0, 1), (1, 0)]


def product(left_side, right_side):
    return jnp.dot(left_side, right_side, precision=TOP, preferred_element_type=jnp.float32)


def inner_product(left_side, right_side):
    return lax.dot_general(
        left_side,
        right_side,
        (((0,), (0,)), ((), ())),
        precision=TOP,
        preferred_element_type=jnp.float32,
    )


def outer_product(left_side, right_side):
    return lax.dot_general(
        left_side,
        right_side,
        (((1,), (1,)), ((), ())),
        precision=TOP,
        preferred_element_type=jnp.float32,
    )


def eliminate(gram):
    n = gram.shape[0]
    count = n // 8
    tile = (8, n)
    row = lax.broadcasted_iota(jnp.int32, tile, 0)
    lane = lax.broadcasted_iota(jnp.int32, tile, 1)
    left = [gram[8 * u : 8 * u + 8, :] for u in range(count)]
    right = [jnp.where(lane == row + 8 * u, 1.0, 0.0).astype(jnp.float32) for u in range(count)]
    for v in range(count):
        start = 8 * v
        rows = [jnp.broadcast_to(left[v][i : i + 1, :], tile) for i in range(PANEL)]
        more = [jnp.broadcast_to(right[v][i : i + 1, :], tile) for i in range(PANEL)]
        columns = [
            [jnp.broadcast_to(left[u][:, start + i : start + i + 1], tile) for u in range(v, count)]
            for i in range(PANEL)
        ]
        corner = [
            [jnp.broadcast_to(rows[i][:, start + m : start + m + 1], tile) for m in range(PANEL)]
            for i in range(PANEL)
        ]
        factors = []
        for i in range(PANEL):
            inverse = 1.0 / corner[i][i]
            factor = [c * inverse for c in columns[i]]
            for m in range(i + 1, PANEL):
                weight = corner[i][m] * inverse
                for q in range(m, PANEL):
                    corner[m][q] = corner[m][q] - weight * corner[i][q]
                rows[m] = rows[m] - weight * rows[i]
                more[m] = more[m] - weight * more[i]
                columns[m] = [c - f * corner[i][m] for c, f in zip(columns[m], factor)]
            factor[0] = jnp.where(row > i, factor[0], 0.0)
            factors.append(factor)
        for u in range(v, count):
            a, b = left[u], right[u]
            for i in range(PANEL):
                a = a - factors[i][u - v] * rows[i]
                b = b - factors[i][u - v] * more[i]
            left[u], right[u] = a, b
    upper, inverse = [], []
    for u in range(count):
        pivots = jnp.sum(jnp.where(lane == row + 8 * u, left[u], 0.0), axis=1, keepdims=True)
        scale = lax.rsqrt(pivots)
        upper.append(jnp.where(lane >= row + 8 * u, left[u] * scale, 0.0))
        inverse.append(right[u] * scale)
    return jnp.concatenate(upper, 0), jnp.concatenate(inverse, 0)


def factor_kernel(gram_ref, upper_ref, inverse_ref):
    upper_ref[...], inverse_ref[...] = eliminate(gram_ref[...])


def factor(gram_matrix):
    like = jax.ShapeDtypeStruct(gram_matrix.shape, jnp.float32)
    return pl.pallas_call(
        factor_kernel,
        out_shape=[like, like],
        name="factor",
        cost_estimate=pl.CostEstimate(flops=20_000_000, bytes_accessed=200_000, transcendentals=0),
    )(gram_matrix)


def scatter_sum(parts, axis):
    return jnp.sum(lax.all_to_all(parts, axis, 0, 0), axis=0)


def gather(block, axis):
    count = lax.axis_size(axis)
    return lax.all_to_all(jnp.broadcast_to(block[None], (count,) + block.shape), axis, 0, 0)


def take(array, index, axis):
    return lax.dynamic_index_in_dim(array, index, axis, keepdims=False)


def per_device(activations, sketch):
    row_count, column_count = activations.shape
    width = sketch.shape[1]
    core = lax.axis_index("core")
    side = lax.axis_index("x_lo")
    plane = ("y", "x_hi")
    plane_count = lax.axis_size("y") * lax.axis_size("x_hi")
    z_count = lax.axis_size("z")
    row_block = row_count // (2 * plane_count)
    half = column_count // 2
    parts = product(activations, sketch).reshape(plane_count, 2, row_block, width)
    received = lax.ppermute(take(parts, 1 - core, 1), "core", SWAP)
    image_block = scatter_sum(take(parts, core, 1) + received, plane)
    mine = gather(image_block, plane)
    other = lax.ppermute(mine, "core", SWAP)
    is_first = core == 0
    image = jnp.stack([jnp.where(is_first, mine, other), jnp.where(is_first, other, mine)], axis=1)
    image = image.reshape(row_count, width)
    back_part = inner_product(activations, image).reshape(2, half, width)
    gram_part = inner_product(image, image)
    received = lax.ppermute(jnp.concatenate([take(back_part, 1 - side, 0), gram_part], axis=0), "x_lo", SWAP)
    back_sum = (take(back_part, side, 0) + received[:half]).reshape(z_count, -1, width)
    gram_sum = (gram_part + received[half:]).reshape(z_count, -1, width)
    back_rows = back_sum.shape[1]
    sums = scatter_sum(jnp.concatenate([back_sum, gram_sum], axis=1), "z")
    both = gather(sums, "z")
    gram_first = both[:, back_rows:].reshape(width, width)
    back_mine = both[:, :back_rows].reshape(half, width)
    back_other = lax.ppermute(back_mine, "x_lo", SWAP)
    unused_first, inverse_first = factor(gram_first)
    is_low = side == 0
    back_raw = jnp.concatenate(
        [jnp.where(is_low, back_mine, back_other), jnp.where(is_low, back_other, back_mine)], axis=0
    )
    first_block = outer_product(image_block, inverse_first)
    back_image = outer_product(back_raw, inverse_first)
    parts = product(activations, back_image).reshape(plane_count, 2, row_block, width)
    gram_part = inner_product(back_image, back_image)[None]
    received = lax.ppermute(jnp.concatenate([take(parts, 1 - core, 1), gram_part], axis=0), "core", SWAP)
    gram_part = jnp.broadcast_to(gram_part + received[plane_count:], (plane_count, width, width))
    parts = jnp.concatenate([take(parts, core, 1) + received[:plane_count], gram_part], axis=1)
    sums = scatter_sum(parts, plane)
    unused_back, inverse_back = factor(sums[row_block:])
    range_block = outer_product(sums[:row_block], inverse_back)
    feat = ("y", "x_hi", "core")
    gram_part = inner_product(range_block, range_block).reshape(2 * plane_count, -1, width)
    gram_slice = scatter_sum(gram_part, feat)
    gram_slice = jnp.sum(gather(gram_slice, ("x_lo", "z")), axis=0)
    gram_last = gather(gram_slice, feat).reshape(width, width)
    upper_factor, inverse_last = factor(gram_last)
    range_basis = outer_product(range_block, inverse_last)
    tokens = row_count * lax.axis_size("x_lo") * z_count
    triangle = upper_factor.T / jnp.sqrt(jnp.float32(tokens))
    return (first_block, range_basis, triangle)


def solution(mesh):
    fine = Mesh(mesh.devices.reshape(2, 16, 4, 2, 2), ("x_lo", "z", "y", "x_hi", "core"))
    tok, feat = ("x_lo", "z"), ("y", "x_hi", "core")
    return jax.shard_map(
        per_device,
        mesh=fine,
        in_specs=(P(tok, feat), P(feat, None)),
        out_specs=(P(tok + feat, None), P(tok + feat, None), P()),
        check_vma=False,
    )
```

```python
import jax
import jax.numpy as jnp
from jax import lax
from jax.experimental import pallas as pl
from jax.experimental.pallas import tpu as pltpu
from jax.sharding import Mesh, PartitionSpec as P

PANEL = 8
SWAP = [(0, 1), (1, 0)]
ROWS = 256
PLANE = ("y", "x_hi")
NEAR = ("x_lo", "z_lo")
CROSS = ("x_lo", "y", "x_hi", "core")
BIG = pltpu.CompilerParams(vmem_limit_bytes=40 * 1024 * 1024)


def terms(value):
    first = value.astype(jnp.bfloat16)
    rest = value - first.astype(jnp.float32)
    second = rest.astype(jnp.bfloat16)
    third = (rest - second.astype(jnp.float32)).astype(jnp.bfloat16)
    return first, second, third


def dot(left_side, right_side):
    return lax.dot_general(
        left_side, right_side, (((1,), (0,)), ((), ())), preferred_element_type=jnp.float32
    )


def product_wide(left_side, wide, third):
    n = third.shape[1]
    l1, l2, l3 = terms(left_side)
    p = dot(l1, wide)
    q = dot(l2, wide)
    low = dot(l1, third) + dot(l3, wide[:, :n])
    return p[:, :n] + ((p[:, n:] + q[:, :n]) + (q[:, n:] + low))


def product(left_side, right_side):
    r1, r2, r3 = terms(right_side)
    return product_wide(left_side, jnp.concatenate([r1, r2], axis=1), r3)


def product_tall(left_side, right_side):
    n = left_side.shape[0]
    l1, l2, l3 = terms(left_side)
    r1, r2, r3 = terms(right_side)
    p = dot(jnp.concatenate([l1, l2, l3], axis=0), r1)
    q = dot(jnp.concatenate([l1, l2], axis=0), r2)
    low = (p[2 * n :] + q[n:]) + dot(l1, r3)
    return p[:n] + ((p[n : 2 * n] + q[:n]) + low)


def eliminate(gram):
    n = gram.shape[0]
    count = n // 8
    tile = (8, n)
    row = lax.broadcasted_iota(jnp.int32, tile, 0)
    lane = lax.broadcasted_iota(jnp.int32, tile, 1)
    left = [gram[8 * u : 8 * u + 8, :] for u in range(count)]
    right = [jnp.where(lane == row + 8 * u, 1.0, 0.0).astype(jnp.float32) for u in range(count)]
    for v in range(count):
        start = 8 * v
        rows = [jnp.broadcast_to(left[v][i : i + 1, :], tile) for i in range(PANEL)]
        more = [jnp.broadcast_to(right[v][i : i + 1, :], tile) for i in range(PANEL)]
        columns = [
            [jnp.broadcast_to(left[u][:, start + i : start + i + 1], tile) for u in range(v, count)]
            for i in range(PANEL)
        ]
        corner = [
            [jnp.broadcast_to(rows[i][:, start + m : start + m + 1], tile) for m in range(PANEL)]
            for i in range(PANEL)
        ]
        factors = []
        for i in range(PANEL):
            inverse = 1.0 / corner[i][i]
            factor = [c * inverse for c in columns[i]]
            for m in range(i + 1, PANEL):
                weight = corner[i][m] * inverse
                for q in range(m, PANEL):
                    corner[m][q] = corner[m][q] - weight * corner[i][q]
                rows[m] = rows[m] - weight * rows[i]
                more[m] = more[m] - weight * more[i]
                columns[m] = [c - f * corner[i][m] for c, f in zip(columns[m], factor)]
            factor[0] = jnp.where(row > i, factor[0], 0.0)
            factors.append(factor)
        for u in range(v, count):
            a, b = left[u], right[u]
            for i in range(PANEL):
                a = a - factors[i][u - v] * rows[i]
                b = b - factors[i][u - v] * more[i]
            left[u], right[u] = a, b
    upper, inverse = [], []
    for u in range(count):
        pivots = jnp.sum(jnp.where(lane == row + 8 * u, left[u], 0.0), axis=1, keepdims=True)
        scale = lax.rsqrt(pivots)
        upper.append(jnp.where(lane >= row + 8 * u, left[u] * scale, 0.0))
        inverse.append(right[u] * scale)
    return jnp.concatenate(upper, 0), jnp.concatenate(inverse, 0)


def part_store(core_ref, value, keep_ref, send_ref):
    half = value.shape[0] // 2
    low, high = value[:half], value[half:]
    is_first = core_ref[0] == 0
    keep_ref[...] = jnp.where(is_first, low, high)[None]
    send_ref[...] = jnp.where(is_first, high, low)[None]


def image_kernel(core_ref, a_ref, s_ref, keep_ref, send_ref, wide_ref, third_ref):
    @pl.when(pl.program_id(0) == 0)
    def _():
        s1, s2, s3 = terms(s_ref[...])
        wide_ref[...] = jnp.concatenate([s1, s2], axis=1)
        third_ref[...] = s3

    part_store(core_ref, product_wide(a_ref[...], wide_ref[...], third_ref[...]), keep_ref, send_ref)


def back_kernel(core_ref, a_ref, mine_ref, other_ref, out_ref, back_ref, gram_ref):
    step = pl.program_id(0)

    @pl.when(step == 0)
    def _():
        back_ref[...] = jnp.zeros_like(back_ref)
        gram_ref[...] = jnp.zeros_like(gram_ref)

    is_first = core_ref[0] == 0
    mine, other = mine_ref[0], other_ref[0]
    y = jnp.concatenate([jnp.where(is_first, mine, other), jnp.where(is_first, other, mine)], axis=0)
    turned = y.T
    back_ref[...] += product_tall(turned, a_ref[...])
    gram_ref[...] += product_tall(turned, y)

    @pl.when(step == pl.num_programs(0) - 1)
    def _():
        back, gram = back_ref[...].T, gram_ref[...]
        count = out_ref.shape[0]
        cut, small = back.shape[0] // count, gram.shape[0] // count
        for k in range(count):
            out_ref[k, :cut, :] = back[k * cut : (k + 1) * cut]
            out_ref[k, cut:, :] = gram[k * small : (k + 1) * small]


def range_kernel(
    core_ref, a_ref, both_ref, image_ref, keep_ref, send_ref, gram_ref, first_ref, wide_ref, third_ref
):
    step = pl.program_id(0)

    @pl.when(step == 0)
    def _():
        n = first_ref.shape[1]
        count = both_ref.shape[0]
        small = n // count
        cut = both_ref.shape[1] - small
        gram = jnp.concatenate([both_ref[k, cut:, :] for k in range(count)], axis=0)
        back = jnp.concatenate([both_ref[k, :cut, :] for k in range(count)], axis=0)
        unused, inverse = eliminate(gram)
        i1, i2, i3 = terms(inverse.T)
        wide = jnp.concatenate([i1, i2], axis=1)
        first_ref[...] = product_wide(image_ref[...], wide, i3)
        back = product_wide(back, wide, i3)
        gram_back = product(back.T, back)
        gram_ref[...] = gram_back
        send_ref[send_ref.shape[0] - 1] = gram_back
        b1, b2, b3 = terms(back)
        wide_ref[...] = jnp.concatenate([b1, b2], axis=1)
        third_ref[...] = b3

    value = product_wide(a_ref[...], wide_ref[...], third_ref[...])
    part_store(core_ref, value, keep_ref, send_ref.at[pl.ds(step, 1)])


def last_gram_kernel(parts_ref, range_ref, gram_ref):
    n = range_ref.shape[0]
    total = parts_ref[0]
    for k in range(1, parts_ref.shape[0]):
        total = total + parts_ref[k]
    unused, inverse = eliminate(total[n:])
    block = product(total[:n], inverse.T)
    range_ref[...] = block
    gram_ref[...] = product(block.T, block)


def basis_kernel(tokens, gram_ref, range_ref, basis_ref, triangle_ref):
    upper, inverse = eliminate(gram_ref[...])
    basis_ref[...] = product(range_ref[...], inverse.T)
    triangle_ref[...] = upper.T / jnp.sqrt(jnp.float32(tokens))


def shape(*sizes):
    return jax.ShapeDtypeStruct(sizes, jnp.float32)


def whole(*sizes):
    return pl.BlockSpec(sizes, lambda i, core: (0,) * len(sizes))


def image_parts(core, a, s):
    rows, depth = a.shape
    n, steps = s.shape[1], rows // ROWS
    block = pl.BlockSpec((1, ROWS // 2, n), lambda i, core: (i, 0, 0))
    return pl.pallas_call(
        image_kernel,
        out_shape=[shape(steps, ROWS // 2, n)] * 2,
        grid_spec=pltpu.PrefetchScalarGridSpec(
            num_scalar_prefetch=1,
            grid=(steps,),
            in_specs=[pl.BlockSpec((ROWS, depth), lambda i, core: (i, 0)), whole(depth, n)],
            out_specs=[block, block],
            scratch_shapes=[pltpu.VMEM((depth, 2 * n), jnp.bfloat16), pltpu.VMEM((depth, n), jnp.bfloat16)],
        ),
        compiler_params=BIG,
        name="image_parts",
    )(core, a, s)


def back_parts(core, a, mine, other, count):
    rows, depth = a.shape
    n, steps = mine.shape[2], rows // ROWS
    chunk = (depth + n) // count
    block = pl.BlockSpec((1, ROWS // 2, n), lambda i, core: (i, 0, 0))
    return pl.pallas_call(
        back_kernel,
        out_shape=shape(count, chunk, n),
        grid_spec=pltpu.PrefetchScalarGridSpec(
            num_scalar_prefetch=1,
            grid=(steps,),
            in_specs=[pl.BlockSpec((ROWS, depth), lambda i, core: (i, 0)), block, block],
            out_specs=whole(count, chunk, n),
            scratch_shapes=[pltpu.VMEM((n, depth), jnp.float32), pltpu.VMEM((n, n), jnp.float32)],
        ),
        compiler_params=BIG,
        name="back_parts",
    )(core, a, mine, other)


def range_parts(core, a, both, image_block):
    rows, depth = a.shape
    n, steps = both.shape[2], rows // ROWS
    block = pl.BlockSpec((1, ROWS // 2, n), lambda i, core: (i, 0, 0))
    return pl.pallas_call(
        range_kernel,
        out_shape=[shape(steps, ROWS // 2, n), shape(steps + 1, ROWS // 2, n), shape(n, n), shape(n, n)],
        grid_spec=pltpu.PrefetchScalarGridSpec(
            num_scalar_prefetch=1,
            grid=(steps,),
            in_specs=[pl.BlockSpec((ROWS, depth), lambda i, core: (i, 0)), whole(*both.shape), whole(n, n)],
            out_specs=[block, whole(steps + 1, ROWS // 2, n), whole(n, n), whole(n, n)],
            scratch_shapes=[pltpu.VMEM((depth, 2 * n), jnp.bfloat16), pltpu.VMEM((depth, n), jnp.bfloat16)],
        ),
        compiler_params=BIG,
        name="range_parts",
    )(core, a, both, image_block)


def last_gram(parts):
    n = parts.shape[2]
    return pl.pallas_call(
        last_gram_kernel, out_shape=[shape(n, n)] * 2, compiler_params=BIG, name="last_gram"
    )(parts)


def basis(gram, block, tokens):
    n = gram.shape[0]
    return pl.pallas_call(
        lambda *refs: basis_kernel(tokens, *refs),
        out_shape=[shape(n, n)] * 2,
        compiler_params=BIG,
        name="basis",
    )(gram, block)


def scatter_sum(parts, axis):
    return jnp.sum(lax.all_to_all(parts, axis, 0, 0), axis=0)


def gather(block, axis):
    count = lax.axis_size(axis)
    return lax.all_to_all(jnp.broadcast_to(block[None], (count,) + block.shape), axis, 0, 0)


def per_device(activations, sketch):
    width = sketch.shape[1]
    core = lax.axis_index("core").astype(jnp.int32).reshape(1)
    keep, send = image_parts(core, activations, sketch)
    image_block = scatter_sum(keep + lax.ppermute(send, "core", SWAP), PLANE)
    mine = gather(image_block, PLANE)
    other = lax.ppermute(mine, "core", SWAP)
    parts = back_parts(core, activations, mine, other, lax.axis_size(NEAR))
    sums = scatter_sum(parts, NEAR)
    sums = jnp.sum(gather(sums, "z_hi"), axis=0)
    both = gather(sums, NEAR)
    keep, send, gram_part, first_block = range_parts(core, activations, both, image_block)
    received = lax.ppermute(send, "core", SWAP)
    count = keep.shape[0]
    gram_part = jnp.broadcast_to(gram_part[None] + received[count:], (count, width, width))
    parts = jnp.concatenate([keep + received[:count], gram_part], axis=1)
    range_block, gram_part = last_gram(lax.all_to_all(parts, PLANE, 0, 0))
    gram_slice = scatter_sum(gram_part.reshape(lax.axis_size(CROSS), -1, width), CROSS)
    gram_slice = jnp.sum(gather(gram_slice, ("z_hi", "z_lo")), axis=0)
    gram_last = gather(gram_slice, CROSS).reshape(width, width)
    tokens = activations.shape[0] * lax.axis_size(("x_lo", "z_hi", "z_lo"))
    range_basis, triangle = basis(gram_last, range_block, tokens)
    return (first_block, range_basis, triangle)


def solution(mesh):
    fine = Mesh(mesh.devices.reshape(2, 4, 4, 4, 2, 2), ("x_lo", "z_hi", "z_lo", "y", "x_hi", "core"))
    tok, feat = ("x_lo", "z_hi", "z_lo"), ("y", "x_hi", "core")
    return jax.shard_map(
        per_device,
        mesh=fine,
        in_specs=(P(tok, feat), P(feat, None)),
        out_specs=(P(tok + feat, None), P(tok + feat, None), P()),
        check_vma=False,
    )
```

```python
import jax
import jax.numpy as jnp
from jax import lax
from jax.experimental import pallas as pl
from jax.experimental.pallas import tpu as pltpu
from jax.sharding import Mesh, PartitionSpec as P

PANEL = 8
SWAP = [(0, 1), (1, 0)]
ROWS = 256
PLANE = ("y", "x_hi")
NEAR = ("x_lo", "z_lo")
CROSS = ("x_lo", "y", "x_hi", "core")
BIG = pltpu.CompilerParams(vmem_limit_bytes=61 * 1024 * 1024)
SMALL = pltpu.CompilerParams(vmem_limit_bytes=32 * 1024 * 1024)


def terms(value):
    first = value.astype(jnp.bfloat16)
    rest = value - first.astype(jnp.float32)
    second = rest.astype(jnp.bfloat16)
    third = (rest - second.astype(jnp.float32)).astype(jnp.bfloat16)
    return first, second, third


def dot(left_side, right_side):
    return lax.dot_general(
        left_side, right_side, (((1,), (0,)), ((), ())), preferred_element_type=jnp.float32
    )


def product_wide(left_side, wide, third):
    n = third.shape[1]
    l1, l2, l3 = terms(left_side)
    p = dot(l1, wide)
    q = dot(l2, wide)
    low = dot(l1, third) + dot(l3, wide[:, :n])
    return p[:, :n] + ((p[:, n:] + q[:, :n]) + (q[:, n:] + low))


def product(left_side, right_side):
    r1, r2, r3 = terms(right_side)
    return product_wide(left_side, jnp.concatenate([r1, r2], axis=1), r3)


def product_tall(left_side, right_side):
    n = left_side.shape[0]
    l1, l2, l3 = terms(left_side)
    r1, r2, r3 = terms(right_side)
    p = dot(jnp.concatenate([l1, l2, l3], axis=0), r1)
    q = dot(jnp.concatenate([l1, l2], axis=0), r2)
    low = (p[2 * n :] + q[n:]) + dot(l1, r3)
    return p[:n] + ((p[n : 2 * n] + q[:n]) + low)


def tree(values):
    while len(values) > 1:
        values = [a + b for a, b in zip(values[::2], values[1::2])]
    return values[0]


def eliminate(gram):
    n = gram.shape[0]
    count = n // 8
    tile = (8, n)
    row = lax.broadcasted_iota(jnp.int32, tile, 0)
    lane = lax.broadcasted_iota(jnp.int32, tile, 1)
    left = [gram[8 * u : 8 * u + 8, :] for u in range(count)]
    right = [jnp.where(lane == row + 8 * u, 1.0, 0.0).astype(jnp.float32) for u in range(count)]
    for v in range(count):
        start = 8 * v
        rows = [jnp.broadcast_to(left[v][i : i + 1, :], tile) for i in range(PANEL)]
        more = [jnp.broadcast_to(right[v][i : i + 1, :], tile) for i in range(PANEL)]
        corner = [
            [jnp.broadcast_to(rows[i][:, start + m : start + m + 1], tile) for m in range(PANEL)]
            for i in range(PANEL)
        ]
        scales = []
        for i in range(PANEL):
            scales.append(1.0 / corner[i][i])
            for m in range(i + 1, PANEL):
                weight = corner[i][m] * scales[i]
                for q in range(m, PANEL):
                    corner[m][q] = corner[m][q] - weight * corner[i][q]
                rows[m] = rows[m] - weight * rows[i]
                more[m] = more[m] - weight * more[i]
        for u in range(v, count):
            factors = []
            for i in range(PANEL):
                column = jnp.broadcast_to(left[u][:, start + i : start + i + 1], tile)
                for m in range(i):
                    column = column - factors[m] * corner[m][i]
                factors.append(column * scales[i])
            if u == v:
                factors = [jnp.where(row > i, factors[i], 0.0) for i in range(PANEL)]
            left[u] = left[u] - tree([f * r for f, r in zip(factors, rows)])
            right[u] = right[u] - tree([f * r for f, r in zip(factors, more)])
    upper, inverse = [], []
    for u in range(count):
        pivots = jnp.sum(jnp.where(lane == row + 8 * u, left[u], 0.0), axis=1, keepdims=True)
        scale = lax.rsqrt(pivots)
        upper.append(jnp.where(lane >= row + 8 * u, left[u] * scale, 0.0))
        inverse.append(right[u] * scale)
    return jnp.concatenate(upper, 0), jnp.concatenate(inverse, 0)


def iotas(gram):
    return [lax.broadcasted_iota(jnp.int32, gram.shape, k) for k in range(2)]


def pack(gram):
    half = gram.shape[0] // 2
    top, last = gram[:half], pltpu.roll(gram[half:], half, 1)
    row, lane = iotas(top)
    diagonal = jnp.sum(jnp.where(lane == row, last, 0.0), axis=0, keepdims=True)
    return jnp.where(lane < row, last, top), jnp.broadcast_to(diagonal, (8, gram.shape[1]))


def unpack(packed):
    half = packed.shape[0] - 8
    top, diagonal = packed[:half], packed[half : half + 1]
    row, lane = iotas(top)
    last = jnp.where(lane < row, top, jnp.where(lane == row, diagonal, 0.0))
    whole = jnp.concatenate([jnp.where(lane < row, 0.0, top), pltpu.roll(last, half, 1)], axis=0)
    row, lane = iotas(whole)
    return jnp.where(row == lane, whole, whole + whole.T)


def halves(core_ref, value):
    half = value.shape[0] // 2
    low, high = value[:half], value[half:]
    is_first = core_ref[0] == 0
    return jnp.where(is_first, low, high), jnp.where(is_first, high, low)


def image_kernel(core_ref, a_ref, s_ref, keep_ref, send_ref, wide_ref, third_ref):
    @pl.when(pl.program_id(0) == 0)
    def _():
        s1, s2, s3 = terms(s_ref[...])
        wide_ref[...] = jnp.concatenate([s1, s2], axis=1)
        third_ref[...] = s3

    keep_ref[0], send_ref[0] = halves(core_ref, product_wide(a_ref[...], wide_ref[...], third_ref[...]))


def back_kernel(core_ref, a_ref, mine_ref, other_ref, out_ref, back_ref, gram_ref):
    step = pl.program_id(0)

    @pl.when(step == 0)
    def _():
        back_ref[...] = jnp.zeros_like(back_ref)
        gram_ref[...] = jnp.zeros_like(gram_ref)

    is_first = core_ref[0] == 0
    mine, other = mine_ref[0], other_ref[0]
    y = jnp.concatenate([jnp.where(is_first, mine, other), jnp.where(is_first, other, mine)], axis=0)
    turned = y.T
    back_ref[...] += product_tall(turned, a_ref[...])
    gram_ref[...] += product_tall(turned, y)

    @pl.when(step == pl.num_programs(0) - 1)
    def _():
        back, gram = back_ref[...].T, gram_ref[...]
        count = out_ref.shape[0]
        cut, small = back.shape[0] // count, gram.shape[0] // count
        for k in range(count):
            out_ref[k, :cut, :] = back[k * cut : (k + 1) * cut]
            out_ref[k, cut:, :] = gram[k * small : (k + 1) * small]


def range_kernel(
    core_ref, a_ref, both_ref, image_ref, keep_ref, send_ref, gram_ref, first_ref, wide_ref, third_ref
):
    step = pl.program_id(0)

    @pl.when(step == 0)
    def _():
        n = first_ref.shape[1]
        count = both_ref.shape[0]
        small = n // count
        cut = both_ref.shape[1] - small
        gram = jnp.concatenate([both_ref[k, cut:, :] for k in range(count)], axis=0)
        back = jnp.concatenate([both_ref[k, :cut, :] for k in range(count)], axis=0)
        unused, inverse = eliminate(gram)
        i1, i2, i3 = terms(inverse.T)
        wide = jnp.concatenate([i1, i2], axis=1)
        first_ref[...] = product_wide(image_ref[...], wide, i3)
        back = product_wide(back, wide, i3)
        top, diagonal = pack(product(back.T, back))
        edge = top.shape[0]
        start = send_ref.shape[0] - edge - 8
        gram_ref[:edge] = top
        gram_ref[edge:] = diagonal
        send_ref[start : start + edge] = top
        send_ref[start + edge :] = diagonal
        b1, b2, b3 = terms(back)
        wide_ref[...] = jnp.concatenate([b1, b2], axis=1)
        third_ref[...] = b3

    keep, send = halves(core_ref, product_wide(a_ref[...], wide_ref[...], third_ref[...]))
    keep_ref[0] = keep
    send_ref[pl.ds(pl.multiple_of(step * keep.shape[0], keep.shape[0]), keep.shape[0])] = send


def last_gram_kernel(parts_ref, range_ref, gram_ref):
    n = range_ref.shape[0]
    total = parts_ref[0]
    for k in range(1, parts_ref.shape[0]):
        total = total + parts_ref[k]
    unused, inverse = eliminate(unpack(total[n:]))
    block = product(total[:n], inverse.T)
    range_ref[...] = block
    gram_ref[...] = product(block.T, block)


def basis_kernel(tokens, gram_ref, range_ref, basis_ref, triangle_ref):
    upper, inverse = eliminate(gram_ref[...])
    basis_ref[...] = product(range_ref[...], inverse.T)
    triangle_ref[...] = upper.T / jnp.sqrt(jnp.float32(tokens))


def shape(*sizes):
    return jax.ShapeDtypeStruct(sizes, jnp.float32)


def whole(*sizes):
    return pl.BlockSpec(sizes, lambda i, core: (0,) * len(sizes))


def image_parts(core, a, s):
    rows, depth = a.shape
    n, steps = s.shape[1], rows // ROWS
    block = pl.BlockSpec((1, ROWS // 2, n), lambda i, core: (i, 0, 0))
    return pl.pallas_call(
        image_kernel,
        out_shape=[shape(steps, ROWS // 2, n)] * 2,
        grid_spec=pltpu.PrefetchScalarGridSpec(
            num_scalar_prefetch=1,
            grid=(steps,),
            in_specs=[pl.BlockSpec((ROWS, depth), lambda i, core: (i, 0)), whole(depth, n)],
            out_specs=[block, block],
            scratch_shapes=[pltpu.VMEM((depth, 2 * n), jnp.bfloat16), pltpu.VMEM((depth, n), jnp.bfloat16)],
        ),
        compiler_params=BIG,
        name="image_parts",
    )(core, a, s)


def back_parts(core, a, mine, other, count):
    rows, depth = a.shape
    n, steps = mine.shape[2], rows // ROWS
    chunk = (depth + n) // count
    block = pl.BlockSpec((1, ROWS // 2, n), lambda i, core: (i, 0, 0))
    return pl.pallas_call(
        back_kernel,
        out_shape=shape(count, chunk, n),
        grid_spec=pltpu.PrefetchScalarGridSpec(
            num_scalar_prefetch=1,
            grid=(steps,),
            in_specs=[pl.BlockSpec((ROWS, depth), lambda i, core: (i, 0)), block, block],
            out_specs=whole(count, chunk, n),
            scratch_shapes=[pltpu.VMEM((n, depth), jnp.float32), pltpu.VMEM((n, n), jnp.float32)],
        ),
        compiler_params=BIG,
        name="back_parts",
    )(core, a, mine, other)


def range_parts(core, a, both, image_block):
    rows, depth = a.shape
    n, steps = both.shape[2], rows // ROWS
    packed = n // 2 + 8
    block = pl.BlockSpec((1, ROWS // 2, n), lambda i, core: (i, 0, 0))
    return pl.pallas_call(
        range_kernel,
        out_shape=[shape(steps, ROWS // 2, n), shape(rows // 2 + packed, n), shape(packed, n), shape(n, n)],
        grid_spec=pltpu.PrefetchScalarGridSpec(
            num_scalar_prefetch=1,
            grid=(steps,),
            in_specs=[pl.BlockSpec((ROWS, depth), lambda i, core: (i, 0)), whole(*both.shape), whole(n, n)],
            out_specs=[block, whole(rows // 2 + packed, n), whole(packed, n), whole(n, n)],
            scratch_shapes=[pltpu.VMEM((depth, 2 * n), jnp.bfloat16), pltpu.VMEM((depth, n), jnp.bfloat16)],
        ),
        compiler_params=BIG,
        name="range_parts",
    )(core, a, both, image_block)


def last_gram(parts):
    n = parts.shape[2]
    return pl.pallas_call(
        last_gram_kernel, out_shape=[shape(n, n)] * 2, compiler_params=SMALL, name="last_gram"
    )(parts)


def basis(gram, block, tokens):
    n = gram.shape[0]
    return pl.pallas_call(
        lambda *refs: basis_kernel(tokens, *refs),
        out_shape=[shape(n, n)] * 2,
        compiler_params=SMALL,
        name="basis",
    )(gram, block)


def scatter_sum(parts, axis):
    return jnp.sum(lax.all_to_all(parts, axis, 0, 0), axis=0)


def gather(block, axis):
    count = lax.axis_size(axis)
    return lax.all_to_all(jnp.broadcast_to(block[None], (count,) + block.shape), axis, 0, 0)


def per_device(activations, sketch):
    width = sketch.shape[1]
    core = lax.axis_index("core").astype(jnp.int32).reshape(1)
    keep, send = image_parts(core, activations, sketch)
    image_block = scatter_sum(keep + lax.ppermute(send, "core", SWAP), PLANE)
    mine = gather(image_block, PLANE)
    other = lax.ppermute(mine, "core", SWAP)
    parts = back_parts(core, activations, mine, other, lax.axis_size(NEAR))
    sums = scatter_sum(parts, NEAR)
    sums = jnp.sum(gather(sums, "z_hi"), axis=0)
    both = gather(sums, NEAR)
    keep, send, gram_part, first_block = range_parts(core, activations, both, image_block)
    received = lax.ppermute(send, "core", SWAP)
    count, rows = keep.shape[:2]
    gram_part = gram_part + received[count * rows :]
    gram_part = jnp.broadcast_to(gram_part[None], (count,) + gram_part.shape)
    parts = jnp.concatenate([keep + received[: count * rows].reshape(keep.shape), gram_part], axis=1)
    range_block, gram_part = last_gram(lax.all_to_all(parts, PLANE, 0, 0))
    gram_slice = scatter_sum(gram_part.reshape(lax.axis_size(CROSS), -1, width), CROSS)
    gram_slice = jnp.sum(gather(gram_slice, ("z_hi", "z_lo")), axis=0)
    gram_last = gather(gram_slice, CROSS).reshape(width, width)
    tokens = activations.shape[0] * lax.axis_size(("x_lo", "z_hi", "z_lo"))
    range_basis, triangle = basis(gram_last, range_block, tokens)
    return (first_block, range_basis, triangle)


def solution(mesh):
    fine = Mesh(mesh.devices.reshape(2, 4, 4, 4, 2, 2), ("x_lo", "z_hi", "z_lo", "y", "x_hi", "core"))
    tok, feat = ("x_lo", "z_hi", "z_lo"), ("y", "x_hi", "core")
    return jax.shard_map(
        per_device,
        mesh=fine,
        in_specs=(P(tok, feat), P(feat, None)),
        out_specs=(P(tok + feat, None), P(tok + feat, None), P()),
        check_vma=False,
    )
```

```python
import jax
import jax.numpy as jnp
from jax import lax
from jax.experimental import pallas as pl
from jax.experimental.pallas import tpu as pltpu
from jax.sharding import Mesh, PartitionSpec as P

PANEL = 8
SWAP = [(0, 1), (1, 0)]
ROWS = 256
PLANE = ("y", "x_hi")
NEAR = ("x_lo", "z_lo")
CROSS = ("x_lo", "y", "x_hi", "core")
PARAMS = pltpu.CompilerParams(vmem_limit_bytes=32 * 1024 * 1024)


def terms(value):
    first = value.astype(jnp.bfloat16)
    rest = value - first.astype(jnp.float32)
    second = rest.astype(jnp.bfloat16)
    third = (rest - second.astype(jnp.float32)).astype(jnp.bfloat16)
    return first, second, third


def dot(left_side, right_side):
    return lax.dot_general(
        left_side, right_side, (((1,), (0,)), ((), ())), preferred_element_type=jnp.float32
    )


def product_wide(left_side, wide, third):
    n = third.shape[1]
    l1, l2, l3 = terms(left_side)
    p = dot(l1, wide)
    q = dot(l2, wide)
    low = dot(l1, third) + dot(l3, wide[:, :n])
    return p[:, :n] + ((p[:, n:] + q[:, :n]) + (q[:, n:] + low))


def product(left_side, right_side):
    r1, r2, r3 = terms(right_side)
    return product_wide(left_side, jnp.concatenate([r1, r2], axis=1), r3)


def product_tall(left_side, right_side):
    n = left_side.shape[0]
    l1, l2, l3 = terms(left_side)
    r1, r2, r3 = terms(right_side)
    p = dot(jnp.concatenate([l1, l2, l3], axis=0), r1)
    q = dot(jnp.concatenate([l1, l2], axis=0), r2)
    low = (p[2 * n :] + q[n:]) + dot(l1, r3)
    return p[:n] + ((p[n : 2 * n] + q[:n]) + low)


def tree(values):
    while len(values) > 1:
        values = [a + b for a, b in zip(values[::2], values[1::2])]
    return values[0]


def eliminate(gram):
    n = gram.shape[0]
    count = n // 8
    tile = (8, n)
    row = lax.broadcasted_iota(jnp.int32, tile, 0)
    lane = lax.broadcasted_iota(jnp.int32, tile, 1)
    left = [gram[8 * u : 8 * u + 8, :] for u in range(count)]
    right = [jnp.where(lane == row + 8 * u, 1.0, 0.0).astype(jnp.float32) for u in range(count)]
    for v in range(count):
        start = 8 * v
        rows = [jnp.broadcast_to(left[v][i : i + 1, :], tile) for i in range(PANEL)]
        more = [jnp.broadcast_to(right[v][i : i + 1, :], tile) for i in range(PANEL)]
        corner = [
            [jnp.broadcast_to(rows[i][:, start + m : start + m + 1], tile) for m in range(PANEL)]
            for i in range(PANEL)
        ]
        scales = []
        for i in range(PANEL):
            scales.append(1.0 / corner[i][i])
            for m in range(i + 1, PANEL):
                weight = corner[i][m] * scales[i]
                for q in range(m, PANEL):
                    corner[m][q] = corner[m][q] - weight * corner[i][q]
                rows[m] = rows[m] - weight * rows[i]
                more[m] = more[m] - weight * more[i]
        for u in range(v, count):
            factors = []
            for i in range(PANEL):
                column = jnp.broadcast_to(left[u][:, start + i : start + i + 1], tile)
                for m in range(i):
                    column = column - factors[m] * corner[m][i]
                factors.append(column * scales[i])
            if u == v:
                factors = [jnp.where(row > i, factors[i], 0.0) for i in range(PANEL)]
            left[u] = left[u] - tree([f * r for f, r in zip(factors, rows)])
            right[u] = right[u] - tree([f * r for f, r in zip(factors, more)])
    upper, inverse = [], []
    for u in range(count):
        pivots = jnp.sum(jnp.where(lane == row + 8 * u, left[u], 0.0), axis=1, keepdims=True)
        scale = lax.rsqrt(pivots)
        upper.append(jnp.where(lane >= row + 8 * u, left[u] * scale, 0.0))
        inverse.append(right[u] * scale)
    return jnp.concatenate(upper, 0), jnp.concatenate(inverse, 0)


def iotas(gram):
    return [lax.broadcasted_iota(jnp.int32, gram.shape, k) for k in range(2)]


def pack(gram):
    half = gram.shape[0] // 2
    top, last = gram[:half], pltpu.roll(gram[half:], half, 1)
    row, lane = iotas(top)
    diagonal = jnp.sum(jnp.where(lane == row, last, 0.0), axis=0, keepdims=True)
    return jnp.where(lane < row, last, top), jnp.broadcast_to(diagonal, (8, gram.shape[1]))


def unpack(packed):
    half = packed.shape[0] - 8
    top, diagonal = packed[:half], packed[half : half + 1]
    row, lane = iotas(top)
    last = jnp.where(lane < row, top, jnp.where(lane == row, diagonal, 0.0))
    whole = jnp.concatenate([jnp.where(lane < row, 0.0, top), pltpu.roll(last, half, 1)], axis=0)
    row, lane = iotas(whole)
    return jnp.where(row == lane, whole, whole + whole.T)


def halves(core_ref, value):
    half = value.shape[0] // 2
    low, high = value[:half], value[half:]
    is_first = core_ref[0] == 0
    return jnp.where(is_first, low, high), jnp.where(is_first, high, low)


def start_copies(a_ref, held_ref, semaphores):
    copies = []
    for i in range(a_ref.shape[0] // ROWS):
        rows = pl.ds(i * ROWS, ROWS)
        copies.append(pltpu.make_async_copy(a_ref.at[rows], held_ref.at[rows], semaphores.at[i]))
        copies[i].start()
    return copies


def image_kernel(
    core_ref, a_ref, s_ref, keep_ref, send_ref, held_ref, sketch_ref, sketch_semaphore, semaphores
):
    sketch_copy = pltpu.make_async_copy(s_ref, sketch_ref, sketch_semaphore)
    sketch_copy.start()
    copies = start_copies(a_ref, held_ref, semaphores)
    sketch_copy.wait()
    s1, s2, s3 = terms(sketch_ref[...])
    wide = jnp.concatenate([s1, s2], axis=1)
    for i, copy in enumerate(copies):
        copy.wait()
        value = product_wide(held_ref[i * ROWS : (i + 1) * ROWS], wide, s3)
        keep_ref[i], send_ref[i] = halves(core_ref, value)


def back_kernel(core_ref, a_ref, mine_ref, other_ref, out_ref, held_ref, back_ref, gram_ref, semaphores):
    copies = start_copies(a_ref, held_ref, semaphores)
    is_first = core_ref[0] == 0
    for i, copy in enumerate(copies):
        mine, other = mine_ref[i], other_ref[i]
        y = jnp.concatenate([jnp.where(is_first, mine, other), jnp.where(is_first, other, mine)], axis=0)
        turned = y.T
        gram = product_tall(turned, y)
        copy.wait()
        back = product_tall(turned, held_ref[i * ROWS : (i + 1) * ROWS])
        if i == 0:
            back_ref[...], gram_ref[...] = back, gram
        else:
            back_ref[...] += back
            gram_ref[...] += gram
    back, gram = back_ref[...].T, gram_ref[...]
    count = out_ref.shape[0]
    cut, small = back.shape[0] // count, gram.shape[0] // count
    for k in range(count):
        out_ref[k, :cut, :] = back[k * cut : (k + 1) * cut]
        out_ref[k, cut:, :] = gram[k * small : (k + 1) * small]


def range_kernel(
    core_ref, a_ref, both_ref, image_ref, keep_ref, send_ref, gram_ref, first_ref, held_ref, semaphores
):
    copies = start_copies(a_ref, held_ref, semaphores)
    n = first_ref.shape[1]
    count = both_ref.shape[0]
    small = n // count
    cut = both_ref.shape[1] - small
    gram = jnp.concatenate([both_ref[k, cut:, :] for k in range(count)], axis=0)
    back = jnp.concatenate([both_ref[k, :cut, :] for k in range(count)], axis=0)
    unused, inverse = eliminate(gram)
    i1, i2, i3 = terms(inverse.T)
    wide = jnp.concatenate([i1, i2], axis=1)
    first_ref[...] = product_wide(image_ref[...], wide, i3)
    back = product_wide(back, wide, i3)
    top, diagonal = pack(product(back.T, back))
    edge = top.shape[0]
    start = send_ref.shape[0] - edge - 8
    gram_ref[:edge] = top
    gram_ref[edge:] = diagonal
    send_ref[start : start + edge] = top
    send_ref[start + edge :] = diagonal
    b1, b2, b3 = terms(back)
    wide = jnp.concatenate([b1, b2], axis=1)
    half = ROWS // 2
    for i, copy in enumerate(copies):
        copy.wait()
        value = product_wide(held_ref[i * ROWS : (i + 1) * ROWS], wide, b3)
        keep_ref[i], send_ref[i * half : (i + 1) * half] = halves(core_ref, value)


def last_gram_kernel(parts_ref, range_ref, gram_ref):
    n = range_ref.shape[0]
    total = parts_ref[0]
    for k in range(1, parts_ref.shape[0]):
        total = total + parts_ref[k]
    unused, inverse = eliminate(unpack(total[n:]))
    block = product(total[:n], inverse.T)
    range_ref[...] = block
    gram_ref[...] = product(block.T, block)


def basis_kernel(tokens, gram_ref, range_ref, basis_ref, triangle_ref):
    upper, inverse = eliminate(gram_ref[...])
    basis_ref[...] = product(range_ref[...], inverse.T)
    triangle_ref[...] = upper.T / jnp.sqrt(jnp.float32(tokens))


def shape(*sizes):
    return jax.ShapeDtypeStruct(sizes, jnp.float32)


def reading(kernel, a, others, out_shape, scratch, name):
    places = [pltpu.SMEM, pltpu.HBM] + others
    return pl.pallas_call(
        kernel,
        out_shape=out_shape,
        in_specs=[pl.BlockSpec(memory_space=place) for place in places],
        scratch_shapes=[pltpu.VMEM(a.shape, jnp.float32)]
        + scratch
        + [pltpu.SemaphoreType.DMA((a.shape[0] // ROWS,))],
        compiler_params=PARAMS,
        name=name,
    )


def image_parts(core, a, s):
    parts = shape(a.shape[0] // ROWS, ROWS // 2, s.shape[1])
    scratch = [pltpu.VMEM(s.shape, jnp.float32), pltpu.SemaphoreType.DMA]
    return reading(image_kernel, a, [pltpu.HBM], [parts, parts], scratch, "image_parts")(core, a, s)


def back_parts(core, a, mine, other, count):
    n, depth = mine.shape[2], a.shape[1]
    scratch = [pltpu.VMEM((n, depth), jnp.float32), pltpu.VMEM((n, n), jnp.float32)]
    out_shape = shape(count, (depth + n) // count, n)
    return reading(back_kernel, a, [pltpu.VMEM] * 2, out_shape, scratch, "back_parts")(core, a, mine, other)


def range_parts(core, a, both, image_block):
    rows, n = a.shape[0], both.shape[2]
    packed = n // 2 + 8
    out_shape = [shape(rows // ROWS, ROWS // 2, n), shape(rows // 2 + packed, n), shape(packed, n), shape(n, n)]
    return reading(range_kernel, a, [pltpu.VMEM] * 2, out_shape, [], "range_parts")(core, a, both, image_block)


def last_gram(parts):
    n = parts.shape[2]
    return pl.pallas_call(
        last_gram_kernel, out_shape=[shape(n, n)] * 2, compiler_params=PARAMS, name="last_gram"
    )(parts)


def basis(gram, block, tokens):
    n = gram.shape[0]
    return pl.pallas_call(
        lambda *refs: basis_kernel(tokens, *refs),
        out_shape=[shape(n, n)] * 2,
        compiler_params=PARAMS,
        name="basis",
    )(gram, block)


def scatter_sum(parts, axis):
    return jnp.sum(lax.all_to_all(parts, axis, 0, 0), axis=0)


def gather(block, axis):
    count = lax.axis_size(axis)
    return lax.all_to_all(jnp.broadcast_to(block[None], (count,) + block.shape), axis, 0, 0)


def per_device(activations, sketch):
    width = sketch.shape[1]
    core = lax.axis_index("core").astype(jnp.int32).reshape(1)
    activations = pltpu.with_memory_space_constraint(activations, pltpu.HBM)
    sketch = pltpu.with_memory_space_constraint(sketch, pltpu.HBM)
    keep, send = image_parts(core, activations, sketch)
    image_block = scatter_sum(keep + lax.ppermute(send, "core", SWAP), PLANE)
    mine = gather(image_block, PLANE)
    other = lax.ppermute(mine, "core", SWAP)
    parts = back_parts(core, activations, mine, other, lax.axis_size(NEAR))
    sums = scatter_sum(parts, NEAR)
    sums = jnp.sum(gather(sums, "z_hi"), axis=0)
    both = gather(sums, NEAR)
    keep, send, gram_part, first_block = range_parts(core, activations, both, image_block)
    received = lax.ppermute(send, "core", SWAP)
    count, rows = keep.shape[:2]
    gram_part = gram_part + received[count * rows :]
    gram_part = jnp.broadcast_to(gram_part[None], (count,) + gram_part.shape)
    parts = jnp.concatenate([keep + received[: count * rows].reshape(keep.shape), gram_part], axis=1)
    range_block, gram_part = last_gram(lax.all_to_all(parts, PLANE, 0, 0))
    gram_slice = scatter_sum(gram_part.reshape(lax.axis_size(CROSS), -1, width), CROSS)
    gram_slice = jnp.sum(gather(gram_slice, ("z_hi", "z_lo")), axis=0)
    gram_last = gather(gram_slice, CROSS).reshape(width, width)
    tokens = activations.shape[0] * lax.axis_size(("x_lo", "z_hi", "z_lo"))
    range_basis, triangle = basis(gram_last, range_block, tokens)
    return (first_block, range_basis, triangle)


def solution(mesh):
    fine = Mesh(mesh.devices.reshape(2, 4, 4, 4, 2, 2), ("x_lo", "z_hi", "z_lo", "y", "x_hi", "core"))
    tok, feat = ("x_lo", "z_hi", "z_lo"), ("y", "x_hi", "core")
    return jax.shard_map(
        per_device,
        mesh=fine,
        in_specs=(P(tok, feat), P(feat, None)),
        out_specs=(P(tok + feat, None), P(tok + feat, None), P()),
        check_vma=False,
    )
```

```python
import jax
import jax.numpy as jnp
from jax import lax
from jax.experimental import pallas as pl
from jax.experimental.pallas import tpu as pltpu
from jax.sharding import Mesh, PartitionSpec as P

PANEL = 8
SWAP = [(0, 1), (1, 0)]
ROWS = 256
BLOCK = 1024
FIRST_PANEL = 5
PLANE = ("y", "x_hi")
NEAR = ("x_lo", "z_lo")
CROSS = ("x_lo", "y", "x_hi", "core")
PARAMS = pltpu.CompilerParams(vmem_limit_bytes=32 * 1024 * 1024)


def terms(value):
    first = value.astype(jnp.bfloat16)
    rest = value - first.astype(jnp.float32)
    second = rest.astype(jnp.bfloat16)
    third = (rest - second.astype(jnp.float32)).astype(jnp.bfloat16)
    return first, second, third


def dot(left_side, right_side):
    return lax.dot_general(
        left_side, right_side, (((1,), (0,)), ((), ())), preferred_element_type=jnp.float32
    )


def product_wide(left_side, wide, third):
    n = third.shape[1]
    l1, l2, l3 = terms(left_side)
    p = dot(l1, wide)
    q = dot(l2, wide)
    low = dot(l1, third) + dot(l3, wide[:, :n])
    return p[:, :n] + ((p[:, n:] + q[:, :n]) + (q[:, n:] + low))


def product(left_side, right_side):
    r1, r2, r3 = terms(right_side)
    return product_wide(left_side, jnp.concatenate([r1, r2], axis=1), r3)


def product_tall(left_side, right_side):
    n = left_side.shape[0]
    l1, l2, l3 = terms(left_side)
    r1, r2, r3 = terms(right_side)
    p = dot(jnp.concatenate([l1, l2, l3], axis=0), r1)
    q = dot(jnp.concatenate([l1, l2], axis=0), r2)
    low = (p[2 * n :] + q[n:]) + dot(l1, r3)
    return p[:n] + ((p[n : 2 * n] + q[:n]) + low)


def tree(values):
    while len(values) > 1:
        values = [a + b for a, b in zip(values[::2], values[1::2])]
    return values[0]


def eliminate(gram, between=lambda panel: None):
    n = gram.shape[0]
    count = n // 8
    tile = (8, n)
    row = lax.broadcasted_iota(jnp.int32, tile, 0)
    lane = lax.broadcasted_iota(jnp.int32, tile, 1)
    left = [gram[8 * u : 8 * u + 8, :] for u in range(count)]
    right = [jnp.where(lane == row + 8 * u, 1.0, 0.0).astype(jnp.float32) for u in range(count)]
    for v in range(count):
        start = 8 * v
        rows = [jnp.broadcast_to(left[v][i : i + 1, :], tile) for i in range(PANEL)]
        more = [jnp.broadcast_to(right[v][i : i + 1, :], tile) for i in range(PANEL)]
        corner = [
            [jnp.broadcast_to(rows[i][:, start + m : start + m + 1], tile) for m in range(PANEL)]
            for i in range(PANEL)
        ]
        scales = []
        for i in range(PANEL):
            scales.append(1.0 / corner[i][i])
            for m in range(i + 1, PANEL):
                weight = corner[i][m] * scales[i]
                for q in range(m, PANEL):
                    corner[m][q] = corner[m][q] - weight * corner[i][q]
                rows[m] = rows[m] - weight * rows[i]
                more[m] = more[m] - weight * more[i]
        for u in range(v, count):
            factors = []
            for i in range(PANEL):
                column = jnp.broadcast_to(left[u][:, start + i : start + i + 1], tile)
                for m in range(i):
                    column = column - factors[m] * corner[m][i]
                factors.append(column * scales[i])
            if u == v:
                factors = [jnp.where(row > i, factors[i], 0.0) for i in range(PANEL)]
            left[u] = left[u] - tree([f * r for f, r in zip(factors, rows)])
            right[u] = right[u] - tree([f * r for f, r in zip(factors, more)])
        between(v)
    upper, inverse = [], []
    for u in range(count):
        pivots = jnp.sum(jnp.where(lane == row + 8 * u, left[u], 0.0), axis=1, keepdims=True)
        scale = lax.rsqrt(pivots)
        upper.append(jnp.where(lane >= row + 8 * u, left[u] * scale, 0.0))
        inverse.append(right[u] * scale)
    return jnp.concatenate(upper, 0), jnp.concatenate(inverse, 0)


def iotas(gram):
    return [lax.broadcasted_iota(jnp.int32, gram.shape, k) for k in range(2)]


def pack(gram):
    half = gram.shape[0] // 2
    top, last = gram[:half], pltpu.roll(gram[half:], half, 1)
    row, lane = iotas(top)
    diagonal = jnp.sum(jnp.where(lane == row, last, 0.0), axis=0, keepdims=True)
    return jnp.where(lane < row, last, top), jnp.broadcast_to(diagonal, (8, gram.shape[1]))


def unpack(packed):
    half = packed.shape[0] - 8
    top, diagonal = packed[:half], packed[half : half + 1]
    row, lane = iotas(top)
    last = jnp.where(lane < row, top, jnp.where(lane == row, diagonal, 0.0))
    whole = jnp.concatenate([jnp.where(lane < row, 0.0, top), pltpu.roll(last, half, 1)], axis=0)
    row, lane = iotas(whole)
    return jnp.where(row == lane, whole, whole + whole.T)


def halves(core_ref, value):
    half = ROWS // 2
    is_first = core_ref[0] == 0
    for start in range(0, value.shape[0], ROWS):
        low, high = value[start : start + half], value[start + half : start + ROWS]
        yield jnp.where(is_first, low, high), jnp.where(is_first, high, low)


def start_copies(a_ref, held_ref, semaphores):
    copies = []
    for i in range(a_ref.shape[0] // BLOCK):
        rows = pl.ds(i * BLOCK, BLOCK)
        copies.append(pltpu.make_async_copy(a_ref.at[rows], held_ref.at[rows], semaphores.at[i]))
        copies[i].start()
    return copies


def image_kernel(
    core_ref, a_ref, s_ref, keep_ref, send_ref, held_ref, sketch_ref, sketch_semaphore, semaphores
):
    sketch_copy = pltpu.make_async_copy(s_ref, sketch_ref, sketch_semaphore)
    sketch_copy.start()
    copies = start_copies(a_ref, held_ref, semaphores)
    sketch_copy.wait()
    s1, s2, s3 = terms(sketch_ref[...])
    wide = jnp.concatenate([s1, s2], axis=1)
    for i, copy in enumerate(copies):
        copy.wait()
        value = product_wide(held_ref[i * BLOCK : (i + 1) * BLOCK], wide, s3)
        for k, (keep, send) in enumerate(halves(core_ref, value), i * (BLOCK // ROWS)):
            keep_ref[k], send_ref[k] = keep, send


def back_kernel(core_ref, a_ref, mine_ref, other_ref, out_ref, held_ref, back_ref, gram_ref, semaphores):
    copies = start_copies(a_ref, held_ref, semaphores)
    is_first = core_ref[0] == 0
    for i, copy in enumerate(copies):
        pieces = []
        for k in range(i * (BLOCK // ROWS), (i + 1) * (BLOCK // ROWS)):
            mine, other = mine_ref[k], other_ref[k]
            pieces += [jnp.where(is_first, mine, other), jnp.where(is_first, other, mine)]
        y = jnp.concatenate(pieces, axis=0)
        turned = y.T
        gram = product_tall(turned, y)
        copy.wait()
        back = product_tall(turned, held_ref[i * BLOCK : (i + 1) * BLOCK])
        if i == 0:
            back_ref[...], gram_ref[...] = back, gram
        else:
            back_ref[...] += back
            gram_ref[...] += gram
    back, gram = back_ref[...].T, gram_ref[...]
    count = out_ref.shape[0]
    cut, small = back.shape[0] // count, gram.shape[0] // count
    for k in range(count):
        out_ref[k, :cut, :] = back[k * cut : (k + 1) * cut]
        out_ref[k, cut:, :] = gram[k * small : (k + 1) * small]


def range_kernel(
    core_ref, a_ref, both_ref, image_ref, keep_ref, send_ref, gram_ref, first_ref, turn_ref, held_ref, semaphores
):
    copies = start_copies(a_ref, held_ref, semaphores)
    n = first_ref.shape[1]
    count = both_ref.shape[0]
    small = n // count
    cut = both_ref.shape[1] - small
    gram = jnp.concatenate([both_ref[k, cut:, :] for k in range(count)], axis=0)
    back = jnp.concatenate([both_ref[k, :cut, :] for k in range(count)], axis=0)
    scale = lax.rsqrt(gram[:1, :1])
    b1, b2, b3 = terms(back * scale)
    beside = jnp.concatenate([b1, b2], axis=1)
    half = ROWS // 2

    def between(panel):
        if panel == FIRST_PANEL:
            for copy in copies:
                copy.wait()
        k = panel - FIRST_PANEL
        if 0 <= k < a_ref.shape[0] // ROWS:
            value = product_wide(held_ref[k * ROWS : (k + 1) * ROWS], beside, b3)
            ((keep, send),) = halves(core_ref, value)
            keep_ref[k], send_ref[k * half : (k + 1) * half] = keep, send

    unused, inverse = eliminate(gram, between)
    turn = inverse.T
    i1, i2, i3 = terms(turn)
    wide = jnp.concatenate([i1, i2], axis=1)
    back = product_wide(back, wide, i3)
    top, diagonal = pack(product(back.T, back))
    edge = top.shape[0]
    start = send_ref.shape[0] - edge - 8
    gram_ref[:edge] = top
    gram_ref[edge:] = diagonal
    send_ref[start : start + edge] = top
    send_ref[start + edge :] = diagonal
    first_ref[...] = product_wide(image_ref[...], wide, i3)
    turn_ref[...] = turn * (gram[:1, :1] * scale)


def last_gram_kernel(parts_ref, turn_ref, range_ref, gram_ref):
    n = range_ref.shape[0]
    total = parts_ref[0]
    for k in range(1, parts_ref.shape[0]):
        total = total + parts_ref[k]
    rows = []

    def between(panel):
        if panel == 2:
            rows.append(product(total[:n], turn_ref[...]))

    unused, inverse = eliminate(unpack(total[n:]), between)
    block = product(rows[0], inverse.T)
    range_ref[...] = block
    gram_ref[...] = product(block.T, block)


def basis_kernel(tokens, gram_ref, range_ref, basis_ref, triangle_ref):
    upper, inverse = eliminate(gram_ref[...])
    basis_ref[...] = product(range_ref[...], inverse.T)
    triangle_ref[...] = upper.T / jnp.sqrt(jnp.float32(tokens))


def shape(*sizes):
    return jax.ShapeDtypeStruct(sizes, jnp.float32)


def reading(kernel, a, others, out_shape, scratch, name):
    places = [pltpu.SMEM, pltpu.HBM] + others
    return pl.pallas_call(
        kernel,
        out_shape=out_shape,
        in_specs=[pl.BlockSpec(memory_space=place) for place in places],
        scratch_shapes=[pltpu.VMEM(a.shape, jnp.float32)]
        + scratch
        + [pltpu.SemaphoreType.DMA((a.shape[0] // BLOCK,))],
        compiler_params=PARAMS,
        name=name,
    )


def image_parts(core, a, s):
    parts = shape(a.shape[0] // ROWS, ROWS // 2, s.shape[1])
    scratch = [pltpu.VMEM(s.shape, jnp.float32), pltpu.SemaphoreType.DMA]
    return reading(image_kernel, a, [pltpu.HBM], [parts, parts], scratch, "image_parts")(core, a, s)


def back_parts(core, a, mine, other, count):
    n, depth = mine.shape[2], a.shape[1]
    scratch = [pltpu.VMEM((n, depth), jnp.float32), pltpu.VMEM((n, n), jnp.float32)]
    out_shape = shape(count, (depth + n) // count, n)
    return reading(back_kernel, a, [pltpu.VMEM] * 2, out_shape, scratch, "back_parts")(core, a, mine, other)


def range_parts(core, a, both, image_block):
    rows, n = a.shape[0], both.shape[2]
    packed = n // 2 + 8
    out_shape = [shape(rows // ROWS, ROWS // 2, n), shape(rows // 2 + packed, n), shape(packed, n)]
    out_shape += [shape(n, n)] * 2
    return reading(range_kernel, a, [pltpu.VMEM] * 2, out_shape, [], "range_parts")(core, a, both, image_block)


def last_gram(parts, turn):
    n = parts.shape[2]
    return pl.pallas_call(
        last_gram_kernel, out_shape=[shape(n, n)] * 2, compiler_params=PARAMS, name="last_gram"
    )(parts, turn)


def basis(gram, block, tokens):
    n = gram.shape[0]
    return pl.pallas_call(
        lambda *refs: basis_kernel(tokens, *refs),
        out_shape=[shape(n, n)] * 2,
        compiler_params=PARAMS,
        name="basis",
    )(gram, block)


def scatter_sum(parts, axis):
    return jnp.sum(lax.all_to_all(parts, axis, 0, 0), axis=0)


def gather(block, axis):
    count = lax.axis_size(axis)
    return lax.all_to_all(jnp.broadcast_to(block[None], (count,) + block.shape), axis, 0, 0)


def per_device(activations, sketch):
    width = sketch.shape[1]
    core = lax.axis_index("core").astype(jnp.int32).reshape(1)
    activations = pltpu.with_memory_space_constraint(activations, pltpu.HBM)
    sketch = pltpu.with_memory_space_constraint(sketch, pltpu.HBM)
    keep, send = image_parts(core, activations, sketch)
    image_block = scatter_sum(keep + lax.ppermute(send, "core", SWAP), PLANE)
    mine = gather(image_block, PLANE)
    other = lax.ppermute(mine, "core", SWAP)
    parts = back_parts(core, activations, mine, other, lax.axis_size(NEAR))
    sums = scatter_sum(parts, NEAR)
    sums = jnp.sum(gather(sums, "z_hi"), axis=0)
    both = gather(sums, NEAR)
    keep, send, gram_part, first_block, turn = range_parts(core, activations, both, image_block)
    received = lax.ppermute(send, "core", SWAP)
    count, rows = keep.shape[:2]
    gram_part = gram_part + received[count * rows :]
    gram_part = jnp.broadcast_to(gram_part[None], (count,) + gram_part.shape)
    parts = jnp.concatenate([keep + received[: count * rows].reshape(keep.shape), gram_part], axis=1)
    range_block, gram_part = last_gram(lax.all_to_all(parts, PLANE, 0, 0), turn)
    gram_slice = scatter_sum(gram_part.reshape(lax.axis_size(CROSS), -1, width), CROSS)
    gram_slice = jnp.sum(gather(gram_slice, ("z_hi", "z_lo")), axis=0)
    gram_last = gather(gram_slice, CROSS).reshape(width, width)
    tokens = activations.shape[0] * lax.axis_size(("x_lo", "z_hi", "z_lo"))
    range_basis, triangle = basis(gram_last, range_block, tokens)
    return (first_block, range_basis, triangle)


def solution(mesh):
    fine = Mesh(mesh.devices.reshape(2, 4, 4, 4, 2, 2), ("x_lo", "z_hi", "z_lo", "y", "x_hi", "core"))
    tok, feat = ("x_lo", "z_hi", "z_lo"), ("y", "x_hi", "core")
    return jax.shard_map(
        per_device,
        mesh=fine,
        in_specs=(P(tok, feat), P(feat, None)),
        out_specs=(P(tok + feat, None), P(tok + feat, None), P()),
        check_vma=False,
    )
```

```python
import jax
import jax.numpy as jnp
from jax import lax
from jax.experimental import pallas as pl
from jax.experimental.pallas import tpu as pltpu
from jax.sharding import Mesh, PartitionSpec as P

PANEL = 8
SWAP = [(0, 1), (1, 0)]
ROWS = 256
BLOCK = 1024
FIRST_PANEL = 5
PLANE = ("y", "x_hi")
NEAR = ("x_lo", "z_lo")
CROSS = ("x_lo", "y", "x_hi", "core")
PARAMS = pltpu.CompilerParams(vmem_limit_bytes=32 * 1024 * 1024)


def terms(value):
    first = value.astype(jnp.bfloat16)
    rest = value - first.astype(jnp.float32)
    second = rest.astype(jnp.bfloat16)
    third = (rest - second.astype(jnp.float32)).astype(jnp.bfloat16)
    return first, second, third


def dot(left_side, right_side):
    return lax.dot_general(
        left_side, right_side, (((1,), (0,)), ((), ())), preferred_element_type=jnp.float32
    )


def product_wide(left_side, wide, third):
    n = third.shape[1]
    l1, l2, l3 = terms(left_side)
    p = dot(l1, wide)
    q = dot(l2, wide)
    low = dot(l1, third) + dot(l3, wide[:, :n])
    return p[:, :n] + ((p[:, n:] + q[:, :n]) + (q[:, n:] + low))


def product(left_side, right_side):
    r1, r2, r3 = terms(right_side)
    return product_wide(left_side, jnp.concatenate([r1, r2], axis=1), r3)


def product_tall(left_side, right_side):
    n = left_side.shape[0]
    l1, l2, l3 = terms(left_side)
    r1, r2, r3 = terms(right_side)
    p = dot(jnp.concatenate([l1, l2, l3], axis=0), r1)
    q = dot(jnp.concatenate([l1, l2], axis=0), r2)
    low = (p[2 * n :] + q[n:]) + dot(l1, r3)
    return p[:n] + ((p[n : 2 * n] + q[:n]) + low)


def tree(values):
    while len(values) > 1:
        values = [a + b for a, b in zip(values[::2], values[1::2])]
    return values[0]


def eliminate(gram, left_ref, right_ref, between=lambda panel: None):
    n = gram.shape[0]
    count = n // 8
    tile = (8, n)
    row = lax.broadcasted_iota(jnp.int32, tile, 0)
    lane = lax.broadcasted_iota(jnp.int32, tile, 1)
    left = [gram[8 * u : 8 * u + 8, :] for u in range(count)]
    right = [jnp.where(lane == row + 8 * u, 1.0, 0.0).astype(jnp.float32) for u in range(count)]
    left_ref[:8], right_ref[:8] = left[0], right[0]
    for v in range(count):
        start = 8 * v
        rows = [left_ref[pl.ds(start + i, 8, stride=0), :] for i in range(PANEL)]
        more = [right_ref[pl.ds(start + i, 8, stride=0), :] for i in range(PANEL)]
        corner = [
            [jnp.broadcast_to(rows[i][:, start + m : start + m + 1], tile) for m in range(PANEL)]
            for i in range(PANEL)
        ]
        scales = []
        for i in range(PANEL):
            scales.append(1.0 / corner[i][i])
            for m in range(i + 1, PANEL):
                weight = corner[i][m] * scales[i]
                for q in range(m, PANEL):
                    corner[m][q] = corner[m][q] - weight * corner[i][q]
                rows[m] = rows[m] - weight * rows[i]
                more[m] = more[m] - weight * more[i]
        for u in range(v + 1, count):
            factors = []
            for i in range(PANEL):
                column = jnp.broadcast_to(left[u][:, start + i : start + i + 1], tile)
                for m in range(i):
                    column = column - factors[m] * corner[m][i]
                factors.append(column * scales[i])
            left[u] = left[u] - tree([f * r for f, r in zip(factors, rows)])
            right[u] = right[u] - tree([f * r for f, r in zip(factors, more)])
            if u == v + 1:
                left_ref[8 * u : 8 * u + 8], right_ref[8 * u : 8 * u + 8] = left[u], right[u]
        left[v], right[v] = rows[-1], more[-1]
        for i in range(PANEL - 1):
            left[v] = jnp.where(row == i, rows[i], left[v])
            right[v] = jnp.where(row == i, more[i], right[v])
        between(v)
    upper, inverse = [], []
    for u in range(count):
        pivots = jnp.sum(jnp.where(lane == row + 8 * u, left[u], 0.0), axis=1, keepdims=True)
        scale = lax.rsqrt(pivots)
        upper.append(jnp.where(lane >= row + 8 * u, left[u] * scale, 0.0))
        inverse.append(right[u] * scale)
    return jnp.concatenate(upper, 0), jnp.concatenate(inverse, 0)


def iotas(gram):
    return [lax.broadcasted_iota(jnp.int32, gram.shape, k) for k in range(2)]


def pack(gram):
    half = gram.shape[0] // 2
    top, last = gram[:half], pltpu.roll(gram[half:], half, 1)
    row, lane = iotas(top)
    diagonal = jnp.sum(jnp.where(lane == row, last, 0.0), axis=0, keepdims=True)
    return jnp.where(lane < row, last, top), jnp.broadcast_to(diagonal, (8, gram.shape[1]))


def unpack(packed):
    half = packed.shape[0] - 8
    top, diagonal = packed[:half], packed[half : half + 1]
    row, lane = iotas(top)
    last = jnp.where(lane < row, top, jnp.where(lane == row, diagonal, 0.0))
    whole = jnp.concatenate([jnp.where(lane < row, 0.0, top), pltpu.roll(last, half, 1)], axis=0)
    row, lane = iotas(whole)
    return jnp.where(row == lane, whole, whole + whole.T)


def halves(core_ref, value):
    half = ROWS // 2
    is_first = core_ref[0] == 0
    for start in range(0, value.shape[0], ROWS):
        low, high = value[start : start + half], value[start + half : start + ROWS]
        yield jnp.where(is_first, low, high), jnp.where(is_first, high, low)


def start_copies(a_ref, held_ref, semaphores):
    copies = []
    for i in range(a_ref.shape[0] // BLOCK):
        rows = pl.ds(i * BLOCK, BLOCK)
        copies.append(pltpu.make_async_copy(a_ref.at[rows], held_ref.at[rows], semaphores.at[i]))
        copies[i].start()
    return copies


def image_kernel(
    core_ref, a_ref, s_ref, keep_ref, send_ref, held_ref, sketch_ref, sketch_semaphore, semaphores
):
    sketch_copy = pltpu.make_async_copy(s_ref, sketch_ref, sketch_semaphore)
    sketch_copy.start()
    copies = start_copies(a_ref, held_ref, semaphores)
    sketch_copy.wait()
    s1, s2, s3 = terms(sketch_ref[...])
    wide = jnp.concatenate([s1, s2], axis=1)
    for i, copy in enumerate(copies):
        copy.wait()
        value = product_wide(held_ref[i * BLOCK : (i + 1) * BLOCK], wide, s3)
        for k, (keep, send) in enumerate(halves(core_ref, value), i * (BLOCK // ROWS)):
            keep_ref[k], send_ref[k] = keep, send


def back_kernel(core_ref, a_ref, mine_ref, other_ref, out_ref, held_ref, back_ref, gram_ref, semaphores):
    copies = start_copies(a_ref, held_ref, semaphores)
    is_first = core_ref[0] == 0
    for i, copy in enumerate(copies):
        pieces = []
        for k in range(i * (BLOCK // ROWS), (i + 1) * (BLOCK // ROWS)):
            mine, other = mine_ref[k], other_ref[k]
            pieces += [jnp.where(is_first, mine, other), jnp.where(is_first, other, mine)]
        y = jnp.concatenate(pieces, axis=0)
        turned = y.T
        gram = product_tall(turned, y)
        copy.wait()
        back = product_tall(turned, held_ref[i * BLOCK : (i + 1) * BLOCK])
        if i == 0:
            back_ref[...], gram_ref[...] = back, gram
        else:
            back_ref[...] += back
            gram_ref[...] += gram
    back, gram = back_ref[...].T, gram_ref[...]
    count = out_ref.shape[0]
    cut, small = back.shape[0] // count, gram.shape[0] // count
    for k in range(count):
        out_ref[k, :cut, :] = back[k * cut : (k + 1) * cut]
        out_ref[k, cut:, :] = gram[k * small : (k + 1) * small]


def range_kernel(
    core_ref,
    a_ref,
    both_ref,
    image_ref,
    keep_ref,
    send_ref,
    gram_ref,
    first_ref,
    turn_ref,
    held_ref,
    left_ref,
    right_ref,
    semaphores,
):
    copies = start_copies(a_ref, held_ref, semaphores)
    n = first_ref.shape[1]
    count = both_ref.shape[0]
    small = n // count
    cut = both_ref.shape[1] - small
    gram = jnp.concatenate([both_ref[k, cut:, :] for k in range(count)], axis=0)
    back = jnp.concatenate([both_ref[k, :cut, :] for k in range(count)], axis=0)
    scale = lax.rsqrt(gram[:1, :1])
    b1, b2, b3 = terms(back * scale)
    beside = jnp.concatenate([b1, b2], axis=1)
    half = ROWS // 2

    def between(panel):
        if panel == FIRST_PANEL:
            for copy in copies:
                copy.wait()
        k = panel - FIRST_PANEL
        if 0 <= k < a_ref.shape[0] // ROWS:
            value = product_wide(held_ref[k * ROWS : (k + 1) * ROWS], beside, b3)
            ((keep, send),) = halves(core_ref, value)
            keep_ref[k], send_ref[k * half : (k + 1) * half] = keep, send

    unused, inverse = eliminate(gram, left_ref, right_ref, between)
    turn = inverse.T
    i1, i2, i3 = terms(turn)
    wide = jnp.concatenate([i1, i2], axis=1)
    back = product_wide(back, wide, i3)
    top, diagonal = pack(product(back.T, back))
    edge = top.shape[0]
    start = send_ref.shape[0] - edge - 8
    gram_ref[:edge] = top
    gram_ref[edge:] = diagonal
    send_ref[start : start + edge] = top
    send_ref[start + edge :] = diagonal
    first_ref[...] = product_wide(image_ref[...], wide, i3)
    turn_ref[...] = turn * (gram[:1, :1] * scale)


def last_gram_kernel(parts_ref, turn_ref, range_ref, gram_ref, left_ref, right_ref):
    n = range_ref.shape[0]
    total = parts_ref[0]
    for k in range(1, parts_ref.shape[0]):
        total = total + parts_ref[k]
    rows = []

    def between(panel):
        if panel == 2:
            rows.append(product(total[:n], turn_ref[...]))

    unused, inverse = eliminate(unpack(total[n:]), left_ref, right_ref, between)
    block = product(rows[0], inverse.T)
    range_ref[...] = block
    gram_ref[...] = product(block.T, block)


def basis_kernel(tokens, gram_ref, range_ref, basis_ref, triangle_ref, left_ref, right_ref):
    upper, inverse = eliminate(gram_ref[...], left_ref, right_ref)
    basis_ref[...] = product(range_ref[...], inverse.T)
    triangle_ref[...] = upper.T / jnp.sqrt(jnp.float32(tokens))


def spread(n):
    return [pltpu.VMEM((n + 8, n), jnp.float32)] * 2


def shape(*sizes):
    return jax.ShapeDtypeStruct(sizes, jnp.float32)


def reading(kernel, a, others, out_shape, scratch, name):
    places = [pltpu.SMEM, pltpu.HBM] + others
    return pl.pallas_call(
        kernel,
        out_shape=out_shape,
        in_specs=[pl.BlockSpec(memory_space=place) for place in places],
        scratch_shapes=[pltpu.VMEM(a.shape, jnp.float32)]
        + scratch
        + [pltpu.SemaphoreType.DMA((a.shape[0] // BLOCK,))],
        compiler_params=PARAMS,
        name=name,
    )


def image_parts(core, a, s):
    parts = shape(a.shape[0] // ROWS, ROWS // 2, s.shape[1])
    scratch = [pltpu.VMEM(s.shape, jnp.float32), pltpu.SemaphoreType.DMA]
    return reading(image_kernel, a, [pltpu.HBM], [parts, parts], scratch, "image_parts")(core, a, s)


def back_parts(core, a, mine, other, count):
    n, depth = mine.shape[2], a.shape[1]
    scratch = [pltpu.VMEM((n, depth), jnp.float32), pltpu.VMEM((n, n), jnp.float32)]
    out_shape = shape(count, (depth + n) // count, n)
    return reading(back_kernel, a, [pltpu.VMEM] * 2, out_shape, scratch, "back_parts")(core, a, mine, other)


def range_parts(core, a, both, image_block):
    rows, n = a.shape[0], both.shape[2]
    packed = n // 2 + 8
    out_shape = [shape(rows // ROWS, ROWS // 2, n), shape(rows // 2 + packed, n), shape(packed, n)]
    out_shape += [shape(n, n)] * 2
    return reading(range_kernel, a, [pltpu.VMEM] * 2, out_shape, spread(n), "range_parts")(core, a, both, image_block)


def last_gram(parts, turn):
    n = parts.shape[2]
    return pl.pallas_call(
        last_gram_kernel,
        out_shape=[shape(n, n)] * 2,
        scratch_shapes=spread(n),
        compiler_params=PARAMS,
        name="last_gram",
    )(parts, turn)


def basis(gram, block, tokens):
    n = gram.shape[0]
    return pl.pallas_call(
        lambda *refs: basis_kernel(tokens, *refs),
        out_shape=[shape(n, n)] * 2,
        scratch_shapes=spread(n),
        compiler_params=PARAMS,
        name="basis",
    )(gram, block)


def scatter_sum(parts, axis):
    return jnp.sum(lax.all_to_all(parts, axis, 0, 0), axis=0)


def gather(block, axis):
    count = lax.axis_size(axis)
    return lax.all_to_all(jnp.broadcast_to(block[None], (count,) + block.shape), axis, 0, 0)


def per_device(activations, sketch):
    width = sketch.shape[1]
    core = lax.axis_index("core").astype(jnp.int32).reshape(1)
    activations = pltpu.with_memory_space_constraint(activations, pltpu.HBM)
    sketch = pltpu.with_memory_space_constraint(sketch, pltpu.HBM)
    keep, send = image_parts(core, activations, sketch)
    image_block = scatter_sum(keep + lax.ppermute(send, "core", SWAP), PLANE)
    mine = gather(image_block, PLANE)
    other = lax.ppermute(mine, "core", SWAP)
    parts = back_parts(core, activations, mine, other, lax.axis_size(NEAR))
    sums = scatter_sum(parts, NEAR)
    sums = jnp.sum(gather(sums, "z_hi"), axis=0)
    both = gather(sums, NEAR)
    keep, send, gram_part, first_block, turn = range_parts(core, activations, both, image_block)
    received = lax.ppermute(send, "core", SWAP)
    count, rows = keep.shape[:2]
    gram_part = gram_part + received[count * rows :]
    gram_part = jnp.broadcast_to(gram_part[None], (count,) + gram_part.shape)
    parts = jnp.concatenate([keep + received[: count * rows].reshape(keep.shape), gram_part], axis=1)
    range_block, gram_part = last_gram(lax.all_to_all(parts, PLANE, 0, 0), turn)
    gram_slice = scatter_sum(gram_part.reshape(lax.axis_size(CROSS), -1, width), CROSS)
    gram_slice = jnp.sum(gather(gram_slice, ("z_hi", "z_lo")), axis=0)
    gram_last = gather(gram_slice, CROSS).reshape(width, width)
    tokens = activations.shape[0] * lax.axis_size(("x_lo", "z_hi", "z_lo"))
    range_basis, triangle = basis(gram_last, range_block, tokens)
    return (first_block, range_basis, triangle)


def solution(mesh):
    fine = Mesh(mesh.devices.reshape(2, 4, 4, 4, 2, 2), ("x_lo", "z_hi", "z_lo", "y", "x_hi", "core"))
    tok, feat = ("x_lo", "z_hi", "z_lo"), ("y", "x_hi", "core")
    return jax.shard_map(
        per_device,
        mesh=fine,
        in_specs=(P(tok, feat), P(feat, None)),
        out_specs=(P(tok + feat, None), P(tok + feat, None), P()),
        check_vma=False,
    )
```

```python
import jax
import jax.numpy as jnp
from jax import lax
from jax.experimental import pallas as pl
from jax.experimental.pallas import tpu as pltpu
from jax.sharding import Mesh, PartitionSpec as P

PANEL = 8
SWAP = [(0, 1), (1, 0)]
ROWS = 256
BLOCK = 1024
FIRST_PANEL = 8
PLANE = ("y", "x_hi")
NEAR = ("x_lo", "z_lo")
CROSS = ("x_lo", "y", "x_hi", "core")
PARAMS = pltpu.CompilerParams(vmem_limit_bytes=32 * 1024 * 1024)


def terms(value):
    first = value.astype(jnp.bfloat16)
    rest = value - first.astype(jnp.float32)
    second = rest.astype(jnp.bfloat16)
    third = (rest - second.astype(jnp.float32)).astype(jnp.bfloat16)
    return first, second, third


def dot(left_side, right_side):
    return lax.dot_general(
        left_side, right_side, (((1,), (0,)), ((), ())), preferred_element_type=jnp.float32
    )


def product_wide(left_side, wide, third):
    n = third.shape[1]
    l1, l2, l3 = terms(left_side)
    p = dot(l1, wide)
    q = dot(l2, wide)
    low = dot(l1, third) + dot(l3, wide[:, :n])
    return p[:, :n] + ((p[:, n:] + q[:, :n]) + (q[:, n:] + low))


def product(left_side, right_side):
    r1, r2, r3 = terms(right_side)
    return product_wide(left_side, jnp.concatenate([r1, r2], axis=1), r3)


def product_tall(left_side, right_side):
    n = left_side.shape[0]
    l1, l2, l3 = terms(left_side)
    r1, r2, r3 = terms(right_side)
    p = dot(jnp.concatenate([l1, l2, l3], axis=0), r1)
    q = dot(jnp.concatenate([l1, l2], axis=0), r2)
    low = (p[2 * n :] + q[n:]) + dot(l1, r3)
    return p[:n] + ((p[n : 2 * n] + q[:n]) + low)


def tree(values):
    while len(values) > 1:
        values = [a + b for a, b in zip(values[::2], values[1::2])]
    return values[0]


def eliminate(gram, left_ref, right_ref, between=lambda panel: None):
    corner_ref = left_ref.at[pl.ds(gram.shape[0] + 8, 72)]
    n = gram.shape[0]
    count = n // 8
    tile = (8, n)
    row = lax.broadcasted_iota(jnp.int32, tile, 0)
    lane = lax.broadcasted_iota(jnp.int32, tile, 1)
    left = [gram[8 * u : 8 * u + 8, :] for u in range(count)]
    right = [jnp.where(lane == row + 8 * u, 1.0, 0.0).astype(jnp.float32) for u in range(count)]
    left_ref[:8], right_ref[:8] = left[0], right[0]
    for v in range(count):
        start = 8 * v
        rows = [left_ref[pl.ds(start + i, 8, stride=0), :] for i in range(PANEL)]
        more = [right_ref[pl.ds(start + i, 8, stride=0), :] for i in range(PANEL)]
        for m in range(PANEL):
            corner_ref[8 * m : 8 * m + 8] = jnp.broadcast_to(left[v][:, start + m : start + m + 1], tile)
        corner = [[corner_ref[pl.ds(8 * m + i, 8, stride=0), :] for m in range(PANEL)] for i in range(PANEL)]
        scales = []
        for i in range(PANEL):
            scales.append(1.0 / corner[i][i])
            for m in range(i + 1, PANEL):
                weight = corner[i][m] * scales[i]
                for q in range(m, PANEL):
                    corner[m][q] = corner[m][q] - weight * corner[i][q]
                rows[m] = rows[m] - weight * rows[i]
                more[m] = more[m] - weight * more[i]
        for u in range(v + 1, count):
            factors = []
            for i in range(PANEL):
                column = jnp.broadcast_to(left[u][:, start + i : start + i + 1], tile)
                for m in range(i):
                    column = column - factors[m] * corner[m][i]
                factors.append(column * scales[i])
            left[u] = left[u] - tree([f * r for f, r in zip(factors, rows)])
            right[u] = right[u] - tree([f * r for f, r in zip(factors, more)])
            if u == v + 1:
                left_ref[8 * u : 8 * u + 8], right_ref[8 * u : 8 * u + 8] = left[u], right[u]
        left[v], right[v] = rows[-1], more[-1]
        for i in range(PANEL - 1):
            left[v] = jnp.where(row == i, rows[i], left[v])
            right[v] = jnp.where(row == i, more[i], right[v])
        between(v)
    upper, inverse = [], []
    for u in range(count):
        pivots = jnp.sum(jnp.where(lane == row + 8 * u, left[u], 0.0), axis=1, keepdims=True)
        scale = lax.rsqrt(pivots)
        upper.append(jnp.where(lane >= row + 8 * u, left[u] * scale, 0.0))
        inverse.append(right[u] * scale)
    return jnp.concatenate(upper, 0), jnp.concatenate(inverse, 0)


def iotas(gram):
    return [lax.broadcasted_iota(jnp.int32, gram.shape, k) for k in range(2)]


def pack(gram):
    half = gram.shape[0] // 2
    top, last = gram[:half], pltpu.roll(gram[half:], half, 1)
    row, lane = iotas(top)
    diagonal = jnp.sum(jnp.where(lane == row, last, 0.0), axis=0, keepdims=True)
    return jnp.where(lane < row, last, top), jnp.broadcast_to(diagonal, (8, gram.shape[1]))


def unpack(packed):
    half = packed.shape[0] - 8
    top, diagonal = packed[:half], packed[half : half + 1]
    row, lane = iotas(top)
    last = jnp.where(lane < row, top, jnp.where(lane == row, diagonal, 0.0))
    whole = jnp.concatenate([jnp.where(lane < row, 0.0, top), pltpu.roll(last, half, 1)], axis=0)
    row, lane = iotas(whole)
    return jnp.where(row == lane, whole, whole + whole.T)


def halves(core_ref, value):
    half = ROWS // 2
    is_first = core_ref[0] == 0
    for start in range(0, value.shape[0], ROWS):
        low, high = value[start : start + half], value[start + half : start + ROWS]
        yield jnp.where(is_first, low, high), jnp.where(is_first, high, low)


def start_copies(a_ref, held_ref, semaphores):
    copies = []
    for i in range(a_ref.shape[0] // BLOCK):
        rows = pl.ds(i * BLOCK, BLOCK)
        copies.append(pltpu.make_async_copy(a_ref.at[rows], held_ref.at[rows], semaphores.at[i]))
        copies[i].start()
    return copies


def image_kernel(
    core_ref, a_ref, s_ref, keep_ref, send_ref, held_ref, sketch_ref, sketch_semaphore, semaphores
):
    sketch_copy = pltpu.make_async_copy(s_ref, sketch_ref, sketch_semaphore)
    sketch_copy.start()
    copies = start_copies(a_ref, held_ref, semaphores)
    sketch_copy.wait()
    s1, s2, s3 = terms(sketch_ref[...])
    wide = jnp.concatenate([s1, s2], axis=1)
    for i, copy in enumerate(copies):
        copy.wait()
        value = product_wide(held_ref[i * BLOCK : (i + 1) * BLOCK], wide, s3)
        for k, (keep, send) in enumerate(halves(core_ref, value), i * (BLOCK // ROWS)):
            keep_ref[k], send_ref[k] = keep, send


def back_kernel(core_ref, a_ref, mine_ref, other_ref, out_ref, held_ref, back_ref, gram_ref, semaphores):
    copies = start_copies(a_ref, held_ref, semaphores)
    is_first = core_ref[0] == 0
    for i, copy in enumerate(copies):
        pieces = []
        for k in range(i * (BLOCK // ROWS), (i + 1) * (BLOCK // ROWS)):
            mine, other = mine_ref[k], other_ref[k]
            pieces += [jnp.where(is_first, mine, other), jnp.where(is_first, other, mine)]
        y = jnp.concatenate(pieces, axis=0)
        turned = y.T
        gram = product_tall(turned, y)
        copy.wait()
        back = product_tall(turned, held_ref[i * BLOCK : (i + 1) * BLOCK])
        if i == 0:
            back_ref[...], gram_ref[...] = back, gram
        else:
            back_ref[...] += back
            gram_ref[...] += gram
    back, gram = back_ref[...].T, gram_ref[...]
    count = out_ref.shape[0]
    cut, small = back.shape[0] // count, gram.shape[0] // count
    for k in range(count):
        out_ref[k, :cut, :] = back[k * cut : (k + 1) * cut]
        out_ref[k, cut:, :] = gram[k * small : (k + 1) * small]


def range_kernel(
    core_ref,
    a_ref,
    both_ref,
    keep_ref,
    send_ref,
    gram_ref,
    turn_ref,
    held_ref,
    left_ref,
    right_ref,
    semaphores,
):
    copies = start_copies(a_ref, held_ref, semaphores)
    n = both_ref.shape[2]
    count = both_ref.shape[0]
    small = n // count
    cut = both_ref.shape[1] - small
    gram = jnp.concatenate([both_ref[k, cut:, :] for k in range(count)], axis=0)
    back = jnp.concatenate([both_ref[k, :cut, :] for k in range(count)], axis=0)
    scale = lax.rsqrt(gram[:1, :1])
    b1, b2, b3 = terms(back * scale)
    beside = jnp.concatenate([b1, b2], axis=1)
    half = ROWS // 2

    def between(panel):
        if panel == FIRST_PANEL:
            for copy in copies:
                copy.wait()
        k = panel - FIRST_PANEL
        if 0 <= k < a_ref.shape[0] // ROWS:
            value = product_wide(held_ref[k * ROWS : (k + 1) * ROWS], beside, b3)
            ((keep, send),) = halves(core_ref, value)
            keep_ref[k], send_ref[k * half : (k + 1) * half] = keep, send

    unused, inverse = eliminate(gram, left_ref, right_ref, between)
    turn = inverse.T
    i1, i2, i3 = terms(turn)
    wide = jnp.concatenate([i1, i2], axis=1)
    back = product_wide(back, wide, i3)
    top, diagonal = pack(product(back.T, back))
    edge = top.shape[0]
    start = send_ref.shape[0] - edge - 8
    gram_ref[:edge] = top
    gram_ref[edge:] = diagonal
    send_ref[start : start + edge] = top
    send_ref[start + edge :] = diagonal
    turn_ref[0], turn_ref[1] = turn, turn * (gram[:1, :1] * scale)


def last_gram_kernel(parts_ref, turn_ref, image_ref, range_ref, gram_ref, first_ref, left_ref, right_ref):
    n = range_ref.shape[0]
    total = parts_ref[0]
    for k in range(1, parts_ref.shape[0]):
        total = total + parts_ref[k]
    rows = []

    def between(panel):
        if panel == 2:
            rows.append(product(total[:n], turn_ref[1]))
        if panel == 4:
            first_ref[...] = product(image_ref[...], turn_ref[0])

    unused, inverse = eliminate(unpack(total[n:]), left_ref, right_ref, between)
    block = product(rows[0], inverse.T)
    range_ref[...] = block
    gram_ref[...] = product(block.T, block)


def basis_kernel(tokens, gram_ref, range_ref, basis_ref, triangle_ref, left_ref, right_ref):
    upper, inverse = eliminate(gram_ref[...], left_ref, right_ref)
    basis_ref[...] = product(range_ref[...], inverse.T)
    triangle_ref[...] = upper.T / jnp.sqrt(jnp.float32(tokens))


def spread(n):
    return [pltpu.VMEM((n + 80, n), jnp.float32), pltpu.VMEM((n + 8, n), jnp.float32)]


def shape(*sizes):
    return jax.ShapeDtypeStruct(sizes, jnp.float32)


def reading(kernel, a, others, out_shape, scratch, name):
    places = [pltpu.SMEM, pltpu.HBM] + others
    return pl.pallas_call(
        kernel,
        out_shape=out_shape,
        in_specs=[pl.BlockSpec(memory_space=place) for place in places],
        scratch_shapes=[pltpu.VMEM(a.shape, jnp.float32)]
        + scratch
        + [pltpu.SemaphoreType.DMA((a.shape[0] // BLOCK,))],
        compiler_params=PARAMS,
        name=name,
    )


def image_parts(core, a, s):
    parts = shape(a.shape[0] // ROWS, ROWS // 2, s.shape[1])
    scratch = [pltpu.VMEM(s.shape, jnp.float32), pltpu.SemaphoreType.DMA]
    return reading(image_kernel, a, [pltpu.HBM], [parts, parts], scratch, "image_parts")(core, a, s)


def back_parts(core, a, mine, other, count):
    n, depth = mine.shape[2], a.shape[1]
    scratch = [pltpu.VMEM((n, depth), jnp.float32), pltpu.VMEM((n, n), jnp.float32)]
    out_shape = shape(count, (depth + n) // count, n)
    return reading(back_kernel, a, [pltpu.VMEM] * 2, out_shape, scratch, "back_parts")(core, a, mine, other)


def range_parts(core, a, both):
    rows, n = a.shape[0], both.shape[2]
    packed = n // 2 + 8
    out_shape = [shape(rows // ROWS, ROWS // 2, n), shape(rows // 2 + packed, n), shape(packed, n)]
    out_shape += [shape(2, n, n)]
    return reading(range_kernel, a, [pltpu.VMEM], out_shape, spread(n), "range_parts")(core, a, both)


def last_gram(parts, turn, image_block):
    n = parts.shape[2]
    return pl.pallas_call(
        last_gram_kernel,
        out_shape=[shape(n, n)] * 3,
        scratch_shapes=spread(n),
        compiler_params=PARAMS,
        name="last_gram",
    )(parts, turn, image_block)


def basis(gram, block, tokens):
    n = gram.shape[0]
    return pl.pallas_call(
        lambda *refs: basis_kernel(tokens, *refs),
        out_shape=[shape(n, n)] * 2,
        scratch_shapes=spread(n),
        compiler_params=PARAMS,
        name="basis",
    )(gram, block)


def scatter_sum(parts, axis):
    return jnp.sum(lax.all_to_all(parts, axis, 0, 0), axis=0)


def gather(block, axis):
    count = lax.axis_size(axis)
    return lax.all_to_all(jnp.broadcast_to(block[None], (count,) + block.shape), axis, 0, 0)


def per_device(activations, sketch):
    width = sketch.shape[1]
    core = lax.axis_index("core").astype(jnp.int32).reshape(1)
    activations = pltpu.with_memory_space_constraint(activations, pltpu.HBM)
    sketch = pltpu.with_memory_space_constraint(sketch, pltpu.HBM)
    keep, send = image_parts(core, activations, sketch)
    image_block = scatter_sum(keep + lax.ppermute(send, "core", SWAP), PLANE)
    mine = gather(image_block, PLANE)
    other = lax.ppermute(mine, "core", SWAP)
    parts = back_parts(core, activations, mine, other, lax.axis_size(NEAR))
    sums = scatter_sum(parts, NEAR)
    sums = jnp.sum(gather(sums, "z_hi"), axis=0)
    both = gather(sums, NEAR)
    keep, send, gram_part, turn = range_parts(core, activations, both)
    received = lax.ppermute(send, "core", SWAP)
    count, rows = keep.shape[:2]
    gram_part = gram_part + received[count * rows :]
    gram_part = jnp.broadcast_to(gram_part[None], (count,) + gram_part.shape)
    parts = jnp.concatenate([keep + received[: count * rows].reshape(keep.shape), gram_part], axis=1)
    parts = lax.all_to_all(parts, PLANE, 0, 0)
    range_block, gram_part, first_block = last_gram(parts, turn, image_block)
    gram_slice = scatter_sum(gram_part.reshape(lax.axis_size(CROSS), -1, width), CROSS)
    gram_slice = jnp.sum(gather(gram_slice, ("z_hi", "z_lo")), axis=0)
    gram_last = gather(gram_slice, CROSS).reshape(width, width)
    tokens = activations.shape[0] * lax.axis_size(("x_lo", "z_hi", "z_lo"))
    range_basis, triangle = basis(gram_last, range_block, tokens)
    return (first_block, range_basis, triangle)


def solution(mesh):
    fine = Mesh(mesh.devices.reshape(2, 4, 4, 4, 2, 2), ("x_lo", "z_hi", "z_lo", "y", "x_hi", "core"))
    tok, feat = ("x_lo", "z_hi", "z_lo"), ("y", "x_hi", "core")
    return jax.shard_map(
        per_device,
        mesh=fine,
        in_specs=(P(tok, feat), P(feat, None)),
        out_specs=(P(tok + feat, None), P(tok + feat, None), P()),
        check_vma=False,
    )
```

```python
import jax
import jax.numpy as jnp
from jax import lax
from jax.experimental import pallas as pl
from jax.experimental.pallas import tpu as pltpu
from jax.sharding import Mesh, PartitionSpec as P

PANEL = 8
SWAP = [(0, 1), (1, 0)]
ROWS = 256
BLOCK = 1024
FIRST_PANEL = 8
PLANE = ("y", "x_hi")
NEAR = ("z_lo", "x_lo")
CROSS = ("core", "x_hi", "y", "x_lo")
PARAMS = pltpu.CompilerParams(vmem_limit_bytes=32 * 1024 * 1024)


def terms(value):
    first = value.astype(jnp.bfloat16)
    rest = value - first.astype(jnp.float32)
    second = rest.astype(jnp.bfloat16)
    third = (rest - second.astype(jnp.float32)).astype(jnp.bfloat16)
    return first, second, third


def dot(left_side, right_side):
    return lax.dot_general(
        left_side, right_side, (((1,), (0,)), ((), ())), preferred_element_type=jnp.float32
    )


def product_wide(left_side, wide, third):
    n = third.shape[1]
    l1, l2, l3 = terms(left_side)
    p = dot(l1, wide)
    q = dot(l2, wide)
    low = dot(l1, third) + dot(l3, wide[:, :n])
    return p[:, :n] + ((p[:, n:] + q[:, :n]) + (q[:, n:] + low))


def product(left_side, right_side):
    r1, r2, r3 = terms(right_side)
    return product_wide(left_side, jnp.concatenate([r1, r2], axis=1), r3)


def product_tall(left_side, right_side):
    n = left_side.shape[0]
    l1, l2, l3 = terms(left_side)
    r1, r2, r3 = terms(right_side)
    p = dot(jnp.concatenate([l1, l2, l3], axis=0), r1)
    q = dot(jnp.concatenate([l1, l2], axis=0), r2)
    low = (p[2 * n :] + q[n:]) + dot(l1, r3)
    return p[:n] + ((p[n : 2 * n] + q[:n]) + low)


def tree(values):
    while len(values) > 1:
        values = [a + b for a, b in zip(values[::2], values[1::2])]
    return values[0]


def eliminate(gram, left_ref, right_ref, between=lambda panel: None):
    corner_ref = left_ref.at[pl.ds(gram.shape[0] + 8, 72)]
    n = gram.shape[0]
    count = n // 8
    tile = (8, n)
    row = lax.broadcasted_iota(jnp.int32, tile, 0)
    lane = lax.broadcasted_iota(jnp.int32, tile, 1)
    left = [gram[8 * u : 8 * u + 8, :] for u in range(count)]
    right = [jnp.where(lane == row + 8 * u, 1.0, 0.0).astype(jnp.float32) for u in range(count)]
    left_ref[:8], right_ref[:8] = left[0], right[0]
    for v in range(count):
        start = 8 * v
        rows = [left_ref[pl.ds(start + i, 8, stride=0), :] for i in range(PANEL)]
        more = [right_ref[pl.ds(start + i, 8, stride=0), :] for i in range(PANEL)]
        for m in range(PANEL):
            corner_ref[8 * m : 8 * m + 8] = jnp.broadcast_to(left[v][:, start + m : start + m + 1], tile)
        corner = [[corner_ref[pl.ds(8 * m + i, 8, stride=0), :] for m in range(PANEL)] for i in range(PANEL)]
        scales = []
        for i in range(PANEL):
            scales.append(1.0 / corner[i][i])
            for m in range(i + 1, PANEL):
                weight = corner[i][m] * scales[i]
                for q in range(m, PANEL):
                    corner[m][q] = corner[m][q] - weight * corner[i][q]
                rows[m] = rows[m] - weight * rows[i]
                more[m] = more[m] - weight * more[i]
        for u in range(v + 1, count):
            factors = []
            for i in range(PANEL):
                column = jnp.broadcast_to(left[u][:, start + i : start + i + 1], tile)
                for m in range(i):
                    column = column - factors[m] * corner[m][i]
                factors.append(column * scales[i])
            left[u] = left[u] - tree([f * r for f, r in zip(factors, rows)])
            right[u] = right[u] - tree([f * r for f, r in zip(factors, more)])
            if u == v + 1:
                left_ref[8 * u : 8 * u + 8], right_ref[8 * u : 8 * u + 8] = left[u], right[u]
        left[v], right[v] = rows[-1], more[-1]
        for i in range(PANEL - 1):
            left[v] = jnp.where(row == i, rows[i], left[v])
            right[v] = jnp.where(row == i, more[i], right[v])
        between(v)
    upper, inverse = [], []
    for u in range(count):
        pivots = jnp.sum(jnp.where(lane == row + 8 * u, left[u], 0.0), axis=1, keepdims=True)
        scale = lax.rsqrt(pivots)
        upper.append(jnp.where(lane >= row + 8 * u, left[u] * scale, 0.0))
        inverse.append(right[u] * scale)
    return jnp.concatenate(upper, 0), jnp.concatenate(inverse, 0)


def iotas(gram):
    return [lax.broadcasted_iota(jnp.int32, gram.shape, k) for k in range(2)]


def pack(gram):
    half = gram.shape[0] // 2
    top, last = gram[:half], pltpu.roll(gram[half:], half, 1)
    row, lane = iotas(top)
    diagonal = jnp.sum(jnp.where(lane == row, last, 0.0), axis=0, keepdims=True)
    return jnp.where(lane < row, last, top), jnp.broadcast_to(diagonal, (8, gram.shape[1]))


def unpack(packed):
    half = packed.shape[0] - 8
    top, diagonal = packed[:half], packed[half : half + 1]
    row, lane = iotas(top)
    last = jnp.where(lane < row, top, jnp.where(lane == row, diagonal, 0.0))
    whole = jnp.concatenate([jnp.where(lane < row, 0.0, top), pltpu.roll(last, half, 1)], axis=0)
    row, lane = iotas(whole)
    return jnp.where(row == lane, whole, whole + whole.T)


def halves(core_ref, value):
    half = ROWS // 2
    is_first = core_ref[0] == 0
    for start in range(0, value.shape[0], ROWS):
        low, high = value[start : start + half], value[start + half : start + ROWS]
        yield jnp.where(is_first, low, high), jnp.where(is_first, high, low)


def start_copies(a_ref, held_ref, semaphores):
    copies = []
    for i in range(a_ref.shape[0] // BLOCK):
        rows = pl.ds(i * BLOCK, BLOCK)
        copies.append(pltpu.make_async_copy(a_ref.at[rows], held_ref.at[rows], semaphores.at[i]))
        copies[i].start()
    return copies


def image_kernel(
    core_ref, a_ref, s_ref, keep_ref, send_ref, held_ref, sketch_ref, sketch_semaphore, semaphores
):
    sketch_copy = pltpu.make_async_copy(s_ref, sketch_ref, sketch_semaphore)
    sketch_copy.start()
    copies = start_copies(a_ref, held_ref, semaphores)
    sketch_copy.wait()
    s1, s2, s3 = terms(sketch_ref[...])
    wide = jnp.concatenate([s1, s2], axis=1)
    for i, copy in enumerate(copies):
        copy.wait()
        value = product_wide(held_ref[i * BLOCK : (i + 1) * BLOCK], wide, s3)
        for k, (keep, send) in enumerate(halves(core_ref, value), i * (BLOCK // ROWS)):
            keep_ref[k], send_ref[k] = keep, send


def back_kernel(core_ref, a_ref, mine_ref, other_ref, out_ref, held_ref, back_ref, gram_ref, semaphores):
    copies = start_copies(a_ref, held_ref, semaphores)
    is_first = core_ref[0] == 0
    for i, copy in enumerate(copies):
        pieces = []
        for k in range(i * (BLOCK // ROWS), (i + 1) * (BLOCK // ROWS)):
            mine, other = mine_ref[k], other_ref[k]
            pieces += [jnp.where(is_first, mine, other), jnp.where(is_first, other, mine)]
        y = jnp.concatenate(pieces, axis=0)
        turned = y.T
        gram = product_tall(turned, y)
        copy.wait()
        back = product_tall(turned, held_ref[i * BLOCK : (i + 1) * BLOCK])
        if i == 0:
            back_ref[...], gram_ref[...] = back, gram
        else:
            back_ref[...] += back
            gram_ref[...] += gram
    back, gram = back_ref[...].T, gram_ref[...]
    count = out_ref.shape[0]
    cut, small = back.shape[0] // count, gram.shape[0] // count
    for k in range(count):
        out_ref[k, :cut, :] = back[k * cut : (k + 1) * cut]
        out_ref[k, cut:, :] = gram[k * small : (k + 1) * small]


def range_kernel(
    core_ref,
    a_ref,
    both_ref,
    keep_ref,
    send_ref,
    gram_ref,
    turn_ref,
    held_ref,
    left_ref,
    right_ref,
    semaphores,
):
    copies = start_copies(a_ref, held_ref, semaphores)
    n = both_ref.shape[2]
    count = both_ref.shape[0]
    small = n // count
    cut = both_ref.shape[1] - small
    gram = jnp.concatenate([both_ref[k, cut:, :] for k in range(count)], axis=0)
    back = jnp.concatenate([both_ref[k, :cut, :] for k in range(count)], axis=0)
    scale = lax.rsqrt(gram[:1, :1])
    b1, b2, b3 = terms(back * scale)
    beside = jnp.concatenate([b1, b2], axis=1)
    half = ROWS // 2

    def between(panel):
        if panel == FIRST_PANEL:
            for copy in copies:
                copy.wait()
        k = panel - FIRST_PANEL
        if 0 <= k < a_ref.shape[0] // ROWS:
            value = product_wide(held_ref[k * ROWS : (k + 1) * ROWS], beside, b3)
            ((keep, send),) = halves(core_ref, value)
            keep_ref[k], send_ref[k * half : (k + 1) * half] = keep, send

    unused, inverse = eliminate(gram, left_ref, right_ref, between)
    turn = inverse.T
    i1, i2, i3 = terms(turn)
    wide = jnp.concatenate([i1, i2], axis=1)
    back = product_wide(back, wide, i3)
    top, diagonal = pack(product(back.T, back))
    edge = top.shape[0]
    start = send_ref.shape[0] - edge - 8
    gram_ref[:edge] = top
    gram_ref[edge:] = diagonal
    send_ref[start : start + edge] = top
    send_ref[start + edge :] = diagonal
    turn_ref[0], turn_ref[1] = turn, turn * (gram[:1, :1] * scale)


def last_gram_kernel(parts_ref, turn_ref, image_ref, range_ref, gram_ref, first_ref, left_ref, right_ref):
    n = range_ref.shape[0]
    total = parts_ref[0]
    for k in range(1, parts_ref.shape[0]):
        total = total + parts_ref[k]
    rows = []

    def between(panel):
        if panel == 2:
            rows.append(product(total[:n], turn_ref[1]))
        if panel == 4:
            first_ref[...] = product(image_ref[...], turn_ref[0])

    unused, inverse = eliminate(unpack(total[n:]), left_ref, right_ref, between)
    block = product(rows[0], inverse.T)
    range_ref[...] = block
    gram_ref[...] = product(block.T, block)


def basis_kernel(tokens, gram_ref, range_ref, basis_ref, triangle_ref, left_ref, right_ref):
    upper, inverse = eliminate(gram_ref[...], left_ref, right_ref)
    basis_ref[...] = product(range_ref[...], inverse.T)
    triangle_ref[...] = upper.T / jnp.sqrt(jnp.float32(tokens))


def spread(n):
    return [pltpu.VMEM((n + 80, n), jnp.float32), pltpu.VMEM((n + 8, n), jnp.float32)]


def shape(*sizes):
    return jax.ShapeDtypeStruct(sizes, jnp.float32)


def reading(kernel, a, others, out_shape, scratch, name):
    places = [pltpu.SMEM, pltpu.HBM] + others
    return pl.pallas_call(
        kernel,
        out_shape=out_shape,
        in_specs=[pl.BlockSpec(memory_space=place) for place in places],
        scratch_shapes=[pltpu.VMEM(a.shape, jnp.float32)]
        + scratch
        + [pltpu.SemaphoreType.DMA((a.shape[0] // BLOCK,))],
        compiler_params=PARAMS,
        name=name,
    )


def image_parts(core, a, s):
    parts = shape(a.shape[0] // ROWS, ROWS // 2, s.shape[1])
    scratch = [pltpu.VMEM(s.shape, jnp.float32), pltpu.SemaphoreType.DMA]
    return reading(image_kernel, a, [pltpu.HBM], [parts, parts], scratch, "image_parts")(core, a, s)


def back_parts(core, a, mine, other, count):
    n, depth = mine.shape[2], a.shape[1]
    scratch = [pltpu.VMEM((n, depth), jnp.float32), pltpu.VMEM((n, n), jnp.float32)]
    out_shape = shape(count, (depth + n) // count, n)
    return reading(back_kernel, a, [pltpu.VMEM] * 2, out_shape, scratch, "back_parts")(core, a, mine, other)


def range_parts(core, a, both):
    rows, n = a.shape[0], both.shape[2]
    packed = n // 2 + 8
    out_shape = [shape(rows // ROWS, ROWS // 2, n), shape(rows // 2 + packed, n), shape(packed, n)]
    out_shape += [shape(2, n, n)]
    return reading(range_kernel, a, [pltpu.VMEM], out_shape, spread(n), "range_parts")(core, a, both)


def last_gram(parts, turn, image_block):
    n = parts.shape[2]
    return pl.pallas_call(
        last_gram_kernel,
        out_shape=[shape(n, n)] * 3,
        scratch_shapes=spread(n),
        compiler_params=PARAMS,
        name="last_gram",
    )(parts, turn, image_block)


def basis(gram, block, tokens):
    n = gram.shape[0]
    return pl.pallas_call(
        lambda *refs: basis_kernel(tokens, *refs),
        out_shape=[shape(n, n)] * 2,
        scratch_shapes=spread(n),
        compiler_params=PARAMS,
        name="basis",
    )(gram, block)


def scatter_sum(parts, axis):
    return jnp.sum(lax.all_to_all(parts, axis, 0, 0), axis=0)


def gather(block, axis):
    count = lax.axis_size(axis)
    return lax.all_to_all(jnp.broadcast_to(block[None], (count,) + block.shape), axis, 0, 0)


def per_device(activations, sketch):
    width = sketch.shape[1]
    core = lax.axis_index("core").astype(jnp.int32).reshape(1)
    activations = pltpu.with_memory_space_constraint(activations, pltpu.HBM)
    sketch = pltpu.with_memory_space_constraint(sketch, pltpu.HBM)
    keep, send = image_parts(core, activations, sketch)
    image_block = scatter_sum(keep + lax.ppermute(send, "core", SWAP), PLANE)
    mine = gather(image_block, PLANE)
    other = lax.ppermute(mine, "core", SWAP)
    parts = back_parts(core, activations, mine, other, lax.axis_size(NEAR))
    sums = scatter_sum(parts, NEAR)
    sums = jnp.sum(gather(sums, "z_hi"), axis=0)
    both = gather(sums, NEAR)
    keep, send, gram_part, turn = range_parts(core, activations, both)
    received = lax.ppermute(send, "core", SWAP)
    count, rows = keep.shape[:2]
    gram_part = gram_part + received[count * rows :]
    gram_part = jnp.broadcast_to(gram_part[None], (count,) + gram_part.shape)
    parts = jnp.concatenate([keep + received[: count * rows].reshape(keep.shape), gram_part], axis=1)
    parts = lax.all_to_all(parts, PLANE, 0, 0)
    range_block, gram_part, first_block = last_gram(parts, turn, image_block)
    gram_slice = scatter_sum(gram_part.reshape(lax.axis_size(CROSS), -1, width), CROSS)
    gram_slice = jnp.sum(gather(gram_slice, ("z_hi", "z_lo")), axis=0)
    gram_last = gather(gram_slice, CROSS).reshape(width, width)
    tokens = activations.shape[0] * lax.axis_size(("x_lo", "z_hi", "z_lo"))
    range_basis, triangle = basis(gram_last, range_block, tokens)
    return (first_block, range_basis, triangle)


def solution(mesh):
    fine = Mesh(mesh.devices.reshape(2, 4, 4, 4, 2, 2), ("x_lo", "z_hi", "z_lo", "y", "x_hi", "core"))
    tok, feat = ("x_lo", "z_hi", "z_lo"), ("y", "x_hi", "core")
    return jax.shard_map(
        per_device,
        mesh=fine,
        in_specs=(P(tok, feat), P(feat, None)),
        out_specs=(P(tok + feat, None), P(tok + feat, None), P()),
        check_vma=False,
    )
```
